256 devices in a mesh: pp: 4 (over x_lo, core), dp: 16 (over z, x_hi), tp: 4 (over y).
Axes of the slice: x: 4 (x_hi: 2, x_lo: 2; x = x_hi * 2 + x_lo), y: 4, z: 8, core: 2. Of those that a mesh axis runs over, the one named last changes fastest.
Arguments:
- activations: bfloat16 [4, 2, 2048, 2048], P('pp', None, 'dp'), may hold values from -6 to 6
- upstream_grad: bfloat16 [2, 2048, 2048], P(None, 'dp'), may hold values from -6 to 6
- norm_gain: float32 [4, 2048], P('pp'), may hold values from 0.1 to 1.9
- value_weight: bfloat16 [4, 2048, 2048], P('pp', None, 'tp'), may hold values from -0.125 to 0.125
- gate_weight: bfloat16 [4, 2048, 2048], P('pp', None, 'tp'), may hold values from -0.125 to 0.125
- out_weight: bfloat16 [4, 2048, 2048], P('pp', 'tp'), may hold values from -0.125 to 0.125
- conv_weight: float32 [4, 4, 2048], P('pp', None, 'tp'), may hold values from -3 to 3
Outputs:
- input_grads: bfloat16 [4, 2, 2048, 2048], P('pp', None, ('dp', 'tp'))
- value_grad: float32 [4, 2048, 2048], P('pp', 'dp', 'tp')
- gate_grad: float32 [4, 2048, 2048], P('pp', 'dp', 'tp')
- out_grad: float32 [4, 2048, 2048], P('pp', 'dp', 'tp')
The draws below stay inside these ranges and needn't reach their ends.
All inputs are finite; a program needn't handle non-finite values.
Results may differ from the reference program's by a relative error of at most 0.02.
Values may be sent and summed in bfloat16 or wider, within the bound.
No kernel may reach another device: no remote copies, remote signals or barrier semaphores. Data moves between devices by JAX's collectives and lax.ppermute only.
A program may use at most 128 MiB of HBM per device.

```python
import jax
import jax.numpy as jnp
from jax import lax

D = 2048
VD = 2048
KW = 4
MB = 2
TOK_DEV = 128
TOKENS = 2048
N_PP = 4
N_DP = 16


def strengthened(drawn, rng, source, target, blocks, factor):
    owner, partner = [(jnp.arange(drawn.shape[axis_at]) // (drawn.shape[axis_at] // blocks)).reshape([-1 if axis == axis_at else 1 for axis in range(drawn.ndim)]) for axis_at in (source, target)]
    chosen = jax.random.permutation(rng, blocks)[partner]
    strong = (owner == chosen) | (owner == (partner + blocks // 2) % blocks)
    return jnp.where(strong, factor * drawn, drawn)


def block_levels(stream_key, extent, split, smallest, top_value):
    loudness, own = 1.0, jax.random.fold_in(stream_key, 6)
    for axis_at, blocks in split:
        draws = jnp.exp(jax.random.uniform(jax.random.fold_in(own, axis_at), (blocks,), jnp.float32, smallest / len(split), top_value / len(split)))
        loudness = loudness * jnp.repeat(draws, extent[axis_at] // blocks).reshape([-1 if axis == axis_at else 1 for axis in range(len(extent))])
    return loudness


def noise(key, dims, scale, most, split=(), held_as=jnp.bfloat16):
    entries = scale * jax.random.normal(key, dims, jnp.float32)
    if split:
        entries = entries * block_levels(key, dims, split, -0.22, 0.18)
    return jnp.clip(entries, -most, most).astype(held_as)


def noise_with(rng, shape, deviation, bound, shards, heavy, dtype=jnp.bfloat16):
    entries = deviation * jax.random.normal(rng, shape, jnp.float32)
    if shards:
        entries = entries * block_levels(rng, shape, shards, -0.22, 0.18)
    return jnp.clip(strengthened(entries, jax.random.fold_in(rng, 3), *heavy), -bound, bound).astype(dtype)


def setup_inputs(seed: int = 0) -> dict:
    arg_keys = jax.random.split(jax.random.key(seed), 8)
    return {
        "activations": noise_with(arg_keys[0], (N_PP, MB, TOKENS, D), 1.0, 6.0, ((0, 4), (2, 16)), (2, 3, 16, 2.0)),
        "upstream_grad": noise_with(arg_keys[1], (MB, TOKENS, D), 1.0, 6.0, ((1, 16),), (1, 2, 16, 2.0)),
        "norm_gain": jnp.clip(1.0 + 0.18 * jax.random.normal(arg_keys[2], (N_PP, D), jnp.float32), 0.1, 1.9),
        "value_weight": noise(arg_keys[3], (N_PP, D, VD), D ** -0.5, 0.125, ((0, 4), (2, 4))),
        "gate_weight": noise(arg_keys[4], (N_PP, D, VD), D ** -0.5, 0.125, ((0, 4), (2, 4))),
        "out_weight": noise(arg_keys[5], (N_PP, VD, D), VD ** -0.5, 0.125, ((0, 4), (1, 4))),
        "conv_weight": noise(arg_keys[6], (N_PP, KW, VD), KW ** -0.5, 3.0, ((0, 4), (2, 4)), jnp.float32),
    }


EPSILON = 1e-06

def causal_conv(values, kernel):
    width = kernel.shape[0]
    length = values.shape[-2]
    axis_pos = values.ndim - 2
    pads = [(0, 0)] * (values.ndim - 2) + [(width - 1, 0), (0, 0)]
    padded = jnp.pad(values, pads)
    total = jnp.zeros_like(values)
    for offset in range(width):
        begin = width - 1 - offset
        total = total + kernel[offset] * lax.slice_in_dim(padded, begin, begin + length, axis=axis_pos)
    return total

def conv_adjoint(grads, kernel):
    width = kernel.shape[0]
    length = grads.shape[-2]
    axis_pos = grads.ndim - 2
    pads = [(0, 0)] * (grads.ndim - 2) + [(0, width - 1), (0, 0)]
    padded = jnp.pad(grads, pads)
    total = jnp.zeros_like(grads)
    for offset in range(width):
        total = total + kernel[offset] * lax.slice_in_dim(padded, offset, offset + length, axis=axis_pos)
    return total

def section_back(inputs, upstream, gain, value_w, gate_w, out_w, kernel):
    floats = inputs.astype(jnp.float32)
    inv_rms = lax.rsqrt(lax.optimization_barrier(jnp.mean(floats * floats, axis=-1, keepdims=True)) + EPSILON)
    unit = floats * inv_rms
    normed = (unit * gain).astype(jnp.bfloat16)
    values = jnp.dot(normed, value_w, preferred_element_type=jnp.float32)
    gate_logit = jnp.dot(normed, gate_w, preferred_element_type=jnp.float32)
    channels = values.shape[-1]
    mixed = causal_conv(values.reshape(N_DP, TOK_DEV, channels), kernel).reshape(values.shape)
    sig_mix = jax.nn.sigmoid(mixed)
    act = mixed * sig_mix
    gate = jax.nn.sigmoid(gate_logit)
    hidden = (act * gate).astype(jnp.bfloat16)
    d_hidden = jnp.dot(upstream, out_w.T, preferred_element_type=jnp.float32)
    d_gate = (d_hidden * act * gate * (1.0 - gate)).astype(jnp.bfloat16)
    d_mixed = d_hidden * gate * sig_mix * (1.0 + mixed * (1.0 - sig_mix))
    d_values = conv_adjoint(d_mixed.reshape(N_DP, TOK_DEV, channels), kernel).reshape(values.shape).astype(jnp.bfloat16)
    d_normed = jnp.dot(d_values, value_w.T, preferred_element_type=jnp.float32) + jnp.dot(d_gate, gate_w.T, preferred_element_type=jnp.float32)
    d_unit = d_normed * gain
    d_inputs = upstream.astype(jnp.float32) + inv_rms * (d_unit - unit * lax.optimization_barrier(jnp.mean(d_unit * unit, axis=-1, keepdims=True)))
    grad_value = jnp.dot(normed.T, d_values, preferred_element_type=jnp.float32)
    grad_gate = jnp.dot(normed.T, d_gate, preferred_element_type=jnp.float32)
    grad_out = jnp.dot(upstream.T, hidden, preferred_element_type=jnp.float32)
    return (d_inputs.astype(jnp.bfloat16), grad_value, grad_gate, grad_out)

def reference(activations, upstream_grad, norm_gain, value_weight, gate_weight, out_weight, conv_weight):
    factor = (MB * TOKENS) ** (-0.5)
    carried = upstream_grad
    section_inputs = [None] * N_PP
    value_list = [None] * N_PP
    gate_list = [None] * N_PP
    out_list = [None] * N_PP
    for section in reversed(range(N_PP)):
        new_grads = []
        total_value = jnp.zeros((D, VD), jnp.float32)
        total_gate = jnp.zeros((D, VD), jnp.float32)
        total_out = jnp.zeros((D, VD), jnp.float32)
        for micro in range(MB):
            d_inputs, grad_value, grad_gate, grad_out = section_back(activations[section, micro], carried[micro], norm_gain[section], value_weight[section], gate_weight[section], out_weight[section], conv_weight[section])
            new_grads.append(d_inputs)
            total_value = total_value + grad_value
            total_gate = total_gate + grad_gate
            total_out = total_out + grad_out
        carried = jnp.stack(new_grads)
        section_inputs[section] = carried
        value_list[section] = total_value * factor
        gate_list[section] = total_gate * factor
        out_list[section] = total_out * factor
    return (jnp.stack(section_inputs), jnp.stack(value_list), jnp.stack(gate_list), jnp.stack(out_list))
```

```python
import jax
import jax.numpy as jnp
from jax import lax
from jax.sharding import PartitionSpec as P

EPSILON = 1e-06
F32 = jnp.float32
BF16 = jnp.bfloat16


def causal_conv(values, kernel):
    width, length = kernel.shape[0], values.shape[1]
    padded = jnp.pad(values, ((0, 0), (width - 1, 0), (0, 0)))
    total = kernel[0] * values
    for offset in range(1, width):
        begin = width - 1 - offset
        total = total + kernel[offset] * padded[:, begin:begin + length]
    return total


def conv_adjoint(grads, kernel):
    width, length = kernel.shape[0], grads.shape[1]
    padded = jnp.pad(grads, ((0, 0), (0, width - 1), (0, 0)))
    total = kernel[0] * grads
    for offset in range(1, width):
        total = total + kernel[offset] * padded[:, offset:offset + length]
    return total


def dot(a, b, dims):
    return lax.dot_general(a, b, (dims, ((), ())), preferred_element_type=F32)


def shards(activations, upstream_grad, norm_gain, value_weight, gate_weight, out_weight, conv_weight):
    stored = activations[0]
    gain = norm_gain[0]
    value_w, gate_w, out_w, kernel = value_weight[0], gate_weight[0], out_weight[0], conv_weight[0]
    sections = lax.axis_size("pp")
    section = lax.axis_index("pp")
    tp, tp_index = lax.axis_size("tp"), lax.axis_index("tp")
    dp = lax.axis_size("dp")
    micro, length, width = stored.shape
    rows, share = micro * length, length // tp
    channels = value_w.shape[1]
    factor = (micro * length * dp) ** (-0.5)

    floats = stored.astype(F32)
    inv_rms = lax.rsqrt(jnp.mean(floats * floats, axis=-1, keepdims=True) + EPSILON)
    unit = floats * inv_rms
    normed = (unit * gain).astype(BF16).reshape(rows, width)
    values = dot(normed, value_w, ((1,), (0,)))
    gate_logit = dot(normed, gate_w, ((1,), (0,)))
    mixed = causal_conv(values.reshape(micro, length, channels), kernel).reshape(rows, channels)
    sig_mix = jax.nn.sigmoid(mixed)
    act = mixed * sig_mix
    gate = jax.nn.sigmoid(gate_logit)
    hidden = (act * gate).astype(BF16)
    gate_slope = act * gate * (1.0 - gate)
    mix_slope = gate * sig_mix * (1.0 + mixed * (1.0 - sig_mix))
    own = lambda a: lax.dynamic_slice_in_dim(a, tp_index * share, share, 1)
    unit_rows, inv_rows = own(unit), own(inv_rms)

    upstream = upstream_grad
    d_share = jnp.zeros((micro, share, width), BF16)
    grads = tuple(jnp.zeros((width // dp, channels), F32) for _ in range(3))

    def tick(upstream):
        flat = upstream.reshape(rows, width)
        d_hidden = dot(flat, out_w, ((1,), (1,)))
        d_gate = (d_hidden * gate_slope).astype(BF16)
        d_mixed = (d_hidden * mix_slope).reshape(micro, length, channels)
        d_values = conv_adjoint(d_mixed, kernel).astype(BF16).reshape(rows, channels)
        part = dot(d_values, value_w, ((1,), (1,))) + dot(d_gate, gate_w, ((1,), (1,)))
        blocks = part.astype(BF16).reshape(micro, tp, share, width).transpose(1, 0, 2, 3)
        got = lax.all_to_all(blocks, "tp", 0, 0)
        d_unit = jnp.sum(got.astype(F32), axis=0) * gain
        d_rows = own(upstream).astype(F32) + inv_rows * (d_unit - unit_rows * jnp.mean(d_unit * unit_rows, axis=-1, keepdims=True))
        return d_rows.astype(BF16), d_values, d_gate

    def reduced(upstream, d_values, d_gate):
        flat = upstream.reshape(rows, width)
        parts = [dot(normed, d_values, ((0,), (0,))), dot(normed, d_gate, ((0,), (0,))), dot(flat, hidden, ((0,), (0,)))]
        parts = jnp.stack([p.astype(BF16).reshape(dp, width // dp, channels) for p in parts], axis=1)
        got = lax.all_to_all(parts, "dp", 0, 0)
        total = jnp.sum(got.astype(F32), axis=0) * factor
        return total[0], total[1], total[2]

    def finish(grads, saved):
        up, d_values, d_gate, at = saved
        return lax.cond(
            section == at,
            lambda u, v, g, old: reduced(u, v, g),
            lambda u, v, g, old: old,
            up, d_values, d_gate, grads,
        )

    pending = []
    for at in reversed(range(sections)):
        if at < sections - 1:
            pairs = [(i, i ^ (at ^ (at + 1))) for i in range(sections)]
            arrived = lax.cond(
                (section == at) | (section == at + 1),
                lambda s: lax.ppermute(s, "pp", pairs),
                lambda s: s,
                d_share,
            )
            up, d_values, d_gate, done = pending.pop()
            up, arrived = lax.optimization_barrier((up, arrived))
            grads = finish(grads, (up, d_values, d_gate, done))

            def gathered(arrived, upstream):
                got = lax.all_to_all(jnp.broadcast_to(arrived, (tp,) + arrived.shape), "tp", 0, 0)
                return got.transpose(1, 0, 2, 3).reshape(micro, length, width)
        else:
            arrived = d_share

            def gathered(arrived, upstream):
                return upstream

        def active(arrived, upstream, d_share, grads):
            upstream = gathered(arrived, upstream)
            d_share, d_values, d_gate = tick(upstream)
            return upstream, d_share, d_values, d_gate

        def idle(arrived, upstream, d_share, grads):
            empty = jnp.zeros((rows, channels), BF16)
            return upstream, d_share, empty, empty

        upstream, d_share, d_values, d_gate = lax.cond(section == at, active, idle, arrived, upstream, d_share, grads)
        pending.append((upstream, d_values, d_gate, at))
        if at == 0:
            grads = finish(grads, pending.pop())
    return (d_share[None],) + tuple(g[None] for g in grads)


def solution(mesh):
    placed = (
        P("pp", None, "dp", None), P(None, "dp", None), P("pp", None), P("pp", None, "tp"),
        P("pp", None, "tp"), P("pp", "tp", None), P("pp", None, "tp"),
    )
    return jax.shard_map(
        shards, mesh=mesh, in_specs=placed,
        out_specs=(P("pp", None, ("dp", "tp"), None), P("pp", "dp", "tp"), P("pp", "dp", "tp"), P("pp", "dp", "tp")),
        check_vma=False,
    )
```

```python
import functools

import jax
import jax.numpy as jnp
from jax import lax
from jax.experimental import pallas as pl
from jax.experimental.pallas import tpu as pltpu
from jax.sharding import PartitionSpec as P

EPSILON = 1e-06
F32 = jnp.float32
BF16 = jnp.bfloat16
CHUNK = 256


def dot(a, b, dims):
    return lax.dot_general(a, b, (dims, ((), ())), preferred_element_type=F32)


def in_vmem(kernel, outs, scratch, place, *operands, left_out=(), mib=8):
    whole, where_it_is = pl.BlockSpec(memory_space=pltpu.VMEM), pl.BlockSpec(memory_space=pl.ANY)
    return pl.pallas_call(
        kernel,
        out_shape=outs,
        in_specs=[pl.BlockSpec(memory_space=pltpu.SMEM)] + [where_it_is if n in left_out else whole for n in range(len(operands))],
        out_specs=[whole] * len(outs),
        scratch_shapes=scratch,
        compiler_params=pltpu.CompilerParams(vmem_limit_bytes=mib * 2**20),
    )(place, *operands)


def shape(dims, dtype):
    return jax.ShapeDtypeStruct(dims, dtype)


def row_in_sequence(dims, length):
    return lax.rem(lax.broadcasted_iota(jnp.int32, dims, 0), length)


def pick_columns(source, target, which, block):
    for layer in range(target.shape[1] // block):
        start = pl.multiple_of((2 * layer + which) * block, block)
        target[:, layer * block:(layer + 1) * block] = source[:, pl.ds(start, block)]


def steps(count, body, unroll=True):
    lax.fori_loop(0, count, lambda i, c: (body(i), c)[1], 0, unroll=unroll)


def forward_kernel(block, place, acts, gain, taps, upstream, value_w, gate_w, gate_slope, mix_slope, hidden, keep, send, acts_own, up_own, normed, value_v, gate_v, sems):
    micro, length, width = acts.shape
    share = acts_own.shape[1]
    start = pl.multiple_of(place[0] * share, share)
    copies = [
        pltpu.make_async_copy(value_w, value_v, sems.at[0]),
        pltpu.make_async_copy(gate_w, gate_v, sems.at[1]),
        pltpu.make_async_copy(upstream.at[:, pl.ds(start, share), :], up_own, sems.at[2]),
    ]
    for copy in copies:
        copy.start()
    def normalize(m):
        x = acts[m].astype(F32)
        inv_rms = lax.rsqrt(jnp.mean(x * x, axis=-1, keepdims=True) + EPSILON)
        normed[pl.ds(pl.multiple_of(m * length, length), length), :] = (x * inv_rms * gain[...]).astype(BF16)

    steps(micro, normalize)
    acts_own[...] = acts[:, pl.ds(start, share), :]
    pick_columns(normed, keep, place[1], block)
    pick_columns(normed, send, 1 - place[1], block)
    copies[0].wait()
    copies[1].wait()

    def columns(n):
        cols = pl.ds(pl.multiple_of(n * CHUNK, CHUNK), CHUNK)
        values = dot(normed[...], value_v[:, cols], ((1,), (0,)))
        gate = jax.nn.sigmoid(dot(normed[...], gate_v[:, cols], ((1,), (0,))))
        row = row_in_sequence(values.shape, length)
        mixed = taps[0:1, cols] * values
        for k in range(1, taps.shape[0]):
            mixed = mixed + taps[k:k + 1, cols] * jnp.where(row >= k, pltpu.roll(values, k, 0), 0.0)
        sig_mix = jax.nn.sigmoid(mixed)
        act = mixed * sig_mix
        hidden[:, cols] = (act * gate).astype(BF16)
        gate_slope[:, cols] = act * gate * (1.0 - gate)
        mix_slope[:, cols] = gate * sig_mix * (1.0 + mixed * (1.0 - sig_mix))

    steps(hidden.shape[1] // CHUNK, columns)
    copies[2].wait()


def assemble(place, pieces, up, length):
    micro, share, _ = pieces[0].shape
    tp = len(pieces)
    for k in range(tp):
        at = lax.rem(place[0] - k + tp, tp)
        for m in range(micro):
            start = pl.multiple_of(m * length + at * share, share)
            up[pl.ds(start, share), :] = pieces[k][m]


def pick_kernel(length, block, sides, place, *refs):
    refs, up = refs[:-1], refs[-1]
    given = 1 if len(refs[0].shape) == 3 and refs[0].shape[1] == length else 4
    pieces, outs, rest = refs[:given], refs[given:given + len(sides)], refs[given + len(sides):]
    if given == 1:
        up[...] = pieces[0][...].reshape(up.shape)
    else:
        assemble(place, pieces, up, length)
    for other, out in zip(sides, outs):
        pick_columns(up, out, 1 - place[1] if other else place[1], block)
    for out in rest:
        out[...] = jnp.zeros(out.shape, out.dtype)


def fetch_kernel(place, *refs):
    half = (len(refs) - 1) // 2
    copies = [pltpu.make_async_copy(refs[n], refs[half + n], refs[-1].at[n]) for n in range(half)]
    for copy in copies:
        copy.start()
    for copy in copies:
        copy.wait()


def tick_kernel(whole, length, place, *refs):
    given = 1 if whole else 4
    pieces, refs = refs[:given], refs[given:]
    gate_slope, mix_slope, taps, value_w, gate_w, out_w, both, own, sent1, sent2, sent3, blocks, up, value_v, gate_v, *refs = refs
    *refs, sems = refs
    copies = [pltpu.make_async_copy(value_w, value_v, sems.at[0]), pltpu.make_async_copy(gate_w, gate_v, sems.at[1])]
    if whole:
        out_v, = refs
        copies.insert(0, pltpu.make_async_copy(out_w, out_v, sems.at[2]))
        out_w = out_v
    for copy in copies:
        copy.start()
    tp, micro, share, width = blocks.shape
    rows, channels = gate_slope.shape
    if whole:
        up[...] = pieces[0][...].reshape(rows, width)
        copies.pop(0).wait()
    else:
        assemble(place, pieces, up, length)

    def columns(n):
        start = pl.multiple_of(n * CHUNK, CHUNK)
        cols = pl.ds(start, CHUNK)
        d_hidden = dot(up[...], out_w[cols, :], ((1,), (1,)))
        both[:, pl.ds(pl.multiple_of(channels + start, CHUNK), CHUNK)] = (d_hidden * gate_slope[:, cols]).astype(BF16)
        d_mixed = d_hidden * mix_slope[:, cols]
        row = row_in_sequence(d_mixed.shape, length)
        d_values = taps[0:1, cols] * d_mixed
        for k in range(1, taps.shape[0]):
            d_values = d_values + taps[k:k + 1, cols] * jnp.where(row < length - k, pltpu.roll(d_mixed, rows - k, 0), 0.0)
        both[:, cols] = d_values.astype(BF16)

    steps(channels // CHUNK, columns)
    for copy in copies:
        copy.wait()
    part = 2 * CHUNK

    def inputs(n):
        cols = pl.ds(pl.multiple_of(n * part, part), part)
        d_normed = dot(both[:, :channels], value_v[cols, :], ((1,), (1,))) + dot(both[:, channels:], gate_v[cols, :], ((1,), (1,)))
        d_normed = d_normed.astype(BF16).reshape(micro, tp, share, part)
        for j in range(tp):
            blocks[j, :, :, cols] = d_normed[:, j]

    steps(width // part, inputs)
    for k, out in enumerate((own, sent1, sent2, sent3)):
        out[...] = blocks[lax.rem(place[0] + k, tp)]


def norm_kernel(place, acts, upstream, gain, own, got1, got2, got3, out):
    def sequence(m):
        x = acts[m].astype(F32)
        inv_rms = lax.rsqrt(jnp.mean(x * x, axis=-1, keepdims=True) + EPSILON)
        unit = x * inv_rms
        d_unit = own[m].astype(F32) + got1[m].astype(F32) + got2[m].astype(F32) + got3[m].astype(F32)
        d_unit = d_unit * gain[...]
        mean = jnp.mean(d_unit * unit, axis=-1, keepdims=True)
        out[m] = (upstream[m].astype(F32) + inv_rms * (d_unit - unit * mean)).astype(BF16)

    steps(acts.shape[0], sequence)


def first_kernel(place, n_keep, n_got, both, both_got, u_keep, u_got, hidden, hidden_got, forward, backward):
    block = forward.shape[0]
    layers, channels = n_keep.shape[1] // block, hidden.shape[1]
    for ahead, out in ((layers // 2, forward), (layers // 2 + 1, backward)):
        rows = pl.ds(pl.multiple_of(lax.rem(place[2] + ahead, layers) * block, block), block)
        n_sum = dot(n_keep[:, rows].T, both[...], ((1,), (0,))) + dot(n_got[:, rows].T, both_got[...], ((1,), (0,)))
        u_sum = dot(u_keep[:, rows].T, hidden[...], ((1,), (0,))) + dot(u_got[:, rows].T, hidden_got[...], ((1,), (0,)))
        out[:, :2 * channels] = n_sum.astype(BF16)
        out[:, 2 * channels:] = u_sum.astype(BF16)


def grads_kernel(place, n_keep, n_got, both, both_got, u_keep, u_got, hidden, hidden_got, parts, left):
    layers, block, _ = parts.shape
    rows, channels = hidden.shape

    def products(keep, got, a, a_got, base):
        left[:, :rows] = keep[...].T
        left[:, rows:] = got[...].T

        def columns(n):
            start = pl.multiple_of(n * CHUNK, CHUNK)
            cols = pl.ds(start, CHUNK)
            out = dot(left[:, :rows], a[:, cols], ((1,), (0,))) + dot(left[:, rows:], a_got[:, cols], ((1,), (0,)))
            parts[:, :, pl.ds(pl.multiple_of(base + start, CHUNK), CHUNK)] = out.astype(BF16).reshape(layers, block, CHUNK)

        steps(a.shape[1] // CHUNK, columns, False)

    products(n_keep, n_got, both, both_got, 0)
    products(u_keep, u_got, hidden, hidden_got, 2 * channels)


def ring_kernel(ahead, place, arrived, parts, out):
    layers = parts.shape[0]
    at = lax.rem(place[2] + ahead + layers, layers)
    out[...] = (arrived[...].astype(F32) + parts[at].astype(F32)).astype(BF16)


def close_kernel(factor, place, forward, backward, parts, value, gate, out):
    total = (parts[place[2]].astype(F32) + forward[...].astype(F32) + backward[...].astype(F32)) * factor
    channels = value.shape[1]
    value[...] = total[:, :channels]
    gate[...] = total[:, channels:2 * channels]
    out[...] = total[:, 2 * channels:]


def shards(activations, upstream_grad, norm_gain, value_weight, gate_weight, out_weight, conv_weight):
    acts, taps = activations[0], conv_weight[0]
    value_w, gate_w, out_w = value_weight[0], gate_weight[0], out_weight[0]
    sections, section = lax.axis_size("pp"), lax.axis_index("pp")
    tp, tp_index = lax.axis_size("tp"), lax.axis_index("tp")
    dp, dp_index = lax.axis_size("dp"), lax.axis_index("dp")
    micro, length, width = acts.shape
    channels = value_w.shape[1]
    rows, share, block = micro * length, length // tp, width // dp
    layers = dp // 2
    half = layers * block
    last = sections - 1
    factor = (rows * dp) ** (-0.5)
    place = jnp.stack([tp_index, dp_index % 2, dp_index // 2]).astype(jnp.int32)

    def across(a):
        return lax.ppermute(a, "dp", [(i, i ^ 1) for i in range(dp)])

    def along(a, by):
        return lax.ppermute(a, "dp", [(i, (i + 2 * by) % dp) for i in range(dp)])

    def around(a, by):
        return lax.ppermute(a, "tp", [(i, (i + by) % tp) for i in range(tp)])

    piece = shape((micro, share, width), BF16)
    tokens = shape((rows, channels), BF16)
    side = shape((rows, half), BF16)
    weight = pltpu.VMEM((width, channels), BF16)
    out_weight_v = pltpu.VMEM((channels, width), BF16)
    everything = pltpu.VMEM((rows, width), BF16)
    three = pltpu.SemaphoreType.DMA((3,))

    gate_slope, mix_slope, hidden, n_keep, n_send, acts_own, up_own = in_vmem(
        functools.partial(forward_kernel, block),
        [shape((rows, channels), F32)] * 2 + [tokens, side, side, piece, piece],
        [everything, weight, weight, three],
        place, acts, norm_gain, taps, upstream_grad, value_w, gate_w, left_out=(3, 4, 5), mib=24,
    )

    both_shape = shape((rows, 2 * channels), BF16)

    kept = (out_w, gate_slope, mix_slope, acts_own)

    def fetched():
        return in_vmem(
            fetch_kernel, [shape(a.shape, a.dtype) for a in kept], [pltpu.SemaphoreType.DMA((len(kept),))],
            place, *kept, left_out=range(len(kept)), mib=8,
        )

    def linear(whole, kept, *pieces):
        out_w, gate_slope, mix_slope, _ = kept
        scratch = [pltpu.VMEM((tp,) + piece.shape, BF16), everything, weight, weight] + [out_weight_v] * whole + [three]
        first = len(pieces) + 3
        return in_vmem(
            functools.partial(tick_kernel, whole, length), [both_shape] + [piece] * 4, scratch,
            place, *pieces, gate_slope, mix_slope, taps, value_w, gate_w, out_w,
            left_out=(first, first + 1) + (first + 2,) * whole, mib=24,
        )

    def picked(sides, *pieces, blanks=()):
        return in_vmem(functools.partial(pick_kernel, length, block, sides), [side] * len(sides) + list(blanks), [everything], place, *pieces)

    def gathered(arrived):
        return [arrived] + [around(arrived, k) for k in range(1, tp)]

    def summed(kept, upstream, own, *got):
        return in_vmem(norm_kernel, [piece], [], place, kept[-1], upstream, norm_gain, own, *got)[0]

    def scattered(sent):
        far = around(sent[1], 2)
        return [around(sent[0], 1), far, around(sent[2], 3)]

    def early():
        return across(n_send), across(hidden)

    def blank(like):
        return jnp.zeros(like.shape, BF16)

    def after(a, first):
        return lax.optimization_barrier((a, first))[0]

    def swap(a, flip):
        return lax.ppermute(a, "pp", [(p, p ^ flip) for p in range(sections)])

    def passed_on(at, d_share):
        return lax.cond((section == at) | (section == at + 1), lambda d: swap(d, at ^ (at + 1)), lambda d: blank(d), d_share)

    def begin():
        both, own, *sent = linear(True, kept, upstream_grad)
        got = scattered(sent)
        rest = picked((False, True), after(upstream_grad, own), blanks=(side, tokens))
        return (summed(kept, up_own, own, *got), both, *rest)

    share_3, *state_3, n_got, h_got = lax.cond(
        section == last, begin, lambda: (blank(piece), blank(both_shape), blank(side), blank(side), *early())
    )
    arrived = passed_on(2, share_3)

    def tick(arrived):
        here, pieces = fetched(), gathered(arrived)
        both, own, *sent = linear(False, here, *pieces)
        got = scattered(sent)
        rest = picked((False, True), *after(pieces, own))
        return (summed(here, arrived, own, *got), both, *rest)

    share_2, *state_2 = lax.cond(
        section == 2, tick, lambda a: (blank(piece), blank(both_shape), blank(side), blank(side)), arrived
    )
    arrived = passed_on(1, share_2)

    def closing(arrived, n_got, h_got, *_):
        here, pieces = fetched(), gathered(arrived)
        both, own, *sent = linear(False, here, *pieces)
        got = scattered(sent)
        keep, send = picked((False, True), *after(pieces, own))
        both_got, u_got = across(both), across(send)
        d_share = summed(here, arrived, own, *got)
        return swap(d_share, 1), n_got, h_got, d_share, both, both_got, keep, u_got

    def hand_over(arrived, n_got, h_got, share_2, both_2, keep_2, send_2, share_3, both_3, keep_3, send_3):
        n_got, h_got, d_share, both, keep, send = lax.cond(
            section == last,
            lambda *_: (*early(), share_3, both_3, keep_3, send_3),
            lambda *o: (*o, share_2, both_2, keep_2, send_2),
            n_got, h_got,
        )
        return arrived, n_got, h_got, d_share, both, across(both), keep, across(send)

    arrived, n_got, h_got, *state = lax.cond(
        section < 2, closing, hand_over, arrived, n_got, h_got, share_2, *state_2, share_3, *state_3
    )

    def finish(arrived, *_):
        here, pieces = fetched(), gathered(arrived)
        send, = picked((True,), *pieces)
        u_got = across(send)
        both, own, *sent = linear(False, here, *after(pieces, send))
        both_got = across(both)
        got = scattered(sent)
        keep, = picked((False,), *after(pieces, own))
        return summed(here, arrived, own, *got), both, both_got, keep, u_got

    d_share, both, both_got, u_keep, u_got = lax.cond(section == 0, finish, lambda a, *s: s, arrived, *state)
    factors = (n_keep, n_got, both, both_got, u_keep, u_got, hidden, h_got)
    moving = shape((block, 3 * channels), BF16)
    forward, backward = in_vmem(first_kernel, [moving] * 2, [], place, *factors, mib=12)
    parts, = in_vmem(
        grads_kernel, [shape((layers, block, 3 * channels), BF16)], [pltpu.VMEM((half, 2 * rows), BF16)],
        place, *after(factors, forward), mib=20,
    )
    far, near = layers // 2, layers - 1 - layers // 2
    for step in range(far):
        forward = along(forward, 1)
        if step < far - 1:
            forward = in_vmem(functools.partial(ring_kernel, far - 1 - step), [moving], [], place, forward, parts)[0]
        if step < near:
            backward = along(backward, -1)
        if step < near - 1:
            backward = in_vmem(functools.partial(ring_kernel, step + 1 - near), [moving], [], place, backward, parts)[0]
    grads = in_vmem(
        functools.partial(close_kernel, factor), [shape((block, channels), F32)] * 3, [], place, forward, backward, parts,
    )
    return (d_share[None],) + tuple(g[None] for g in grads)


def solution(mesh):
    placed = (
        P("pp", None, "dp", None), P(None, "dp", None), P("pp", None), P("pp", None, "tp"),
        P("pp", None, "tp"), P("pp", "tp", None), P("pp", None, "tp"),
    )
    return jax.shard_map(
        shards, mesh=mesh, in_specs=placed,
        out_specs=(P("pp", None, ("dp", "tp"), None), P("pp", "dp", "tp"), P("pp", "dp", "tp"), P("pp", "dp", "tp")),
        check_vma=False,
    )
```

```python
import functools

import jax
import jax.numpy as jnp
from jax import lax
from jax.experimental import pallas as pl
from jax.experimental.pallas import tpu as pltpu
from jax.sharding import PartitionSpec as P

EPSILON = 1e-06
F32 = jnp.float32
BF16 = jnp.bfloat16
CHUNK = 256
BIG = 52


def dot(a, b, dims):
    return lax.dot_general(a, b, (dims, ((), ())), preferred_element_type=F32)


def in_vmem(kernel, outs, scratch, place, *operands, left_out=(), mib=8):
    whole, where_it_is = pl.BlockSpec(memory_space=pltpu.VMEM), pl.BlockSpec(memory_space=pltpu.HBM)
    return pl.pallas_call(
        kernel,
        out_shape=outs,
        in_specs=[pl.BlockSpec(memory_space=pltpu.SMEM)] + [where_it_is if n in left_out else whole for n in range(len(operands))],
        out_specs=[whole] * len(outs),
        scratch_shapes=scratch,
        compiler_params=pltpu.CompilerParams(vmem_limit_bytes=mib * 2**20),
    )(place, *operands)


def shape(dims, dtype):
    return jax.ShapeDtypeStruct(dims, dtype)


def row_in_sequence(dims, length):
    return lax.rem(lax.broadcasted_iota(jnp.int32, dims, 0), length)


def pick_columns(source, target, which, block):
    for layer in range(target.shape[1] // block):
        start = pl.multiple_of((2 * layer + which) * block, block)
        target[:, layer * block:(layer + 1) * block] = source[:, pl.ds(start, block)]


def steps(count, body, unroll=True):
    lax.fori_loop(0, count, lambda i, c: (body(i), c)[1], 0, unroll=unroll)


def forward_kernel(block, place, acts_at, gain_at, taps_at, upstream, value_w, gate_w, mine, other, hidden, keep, send, up_mine, up_other, normed, value_v, gate_v, acts, gain, taps, sems):
    micro, length, width = acts.shape
    share, channels = up_mine.shape[1], mine.shape[1]
    start = pl.multiple_of(place[0] * share, share)
    order = (place[3], 1 - place[3])
    first = [
        pltpu.make_async_copy(gain_at, gain, sems.at[4]),
        pltpu.make_async_copy(acts_at.at[order[0]], acts.at[0], sems.at[5]),
        pltpu.make_async_copy(acts_at.at[order[1]], acts.at[1], sems.at[6]),
        pltpu.make_async_copy(taps_at, taps, sems.at[7]),
    ]
    copies = [
        pltpu.make_async_copy(value_w, value_v, sems.at[0]),
        pltpu.make_async_copy(gate_w, gate_v, sems.at[1]),
        pltpu.make_async_copy(upstream.at[order[0], pl.ds(start, share), :], up_mine.at[0], sems.at[2]),
        pltpu.make_async_copy(upstream.at[order[1], pl.ds(start, share), :], up_other.at[0], sems.at[3]),
    ]
    for copy in first + copies:
        copy.start()
    first[0].wait()
    for n, out in enumerate((mine, other)):
        first[1 + n].wait()
        x = acts[n].astype(F32)
        inv_rms = lax.rsqrt(jnp.mean(x * x, axis=-1, keepdims=True) + EPSILON)
        normed[n * length:(n + 1) * length, :] = (x * inv_rms * gain[...]).astype(BF16)
        own = acts[n, pl.ds(start, share), :].astype(F32)
        for k in range(width // channels):
            at = 2 * length + 4 + width // channels + k * share
            out[at:at + share, :] = own[:, k * channels:(k + 1) * channels]
    pick_columns(normed, keep, place[1], block)
    pick_columns(normed, send, 1 - place[1], block)
    for copy in copies[:2] + first[3:]:
        copy.wait()
    for n in range(0, channels, CHUNK):
        cols = slice(n, n + CHUNK)
        values = dot(normed[...], value_v[:, cols], ((1,), (0,)))
        gate = jax.nn.sigmoid(dot(normed[...], gate_v[:, cols], ((1,), (0,))))
        row = row_in_sequence(values.shape, length)
        mixed = taps[0:1, cols] * values
        for k in range(1, taps.shape[0]):
            mixed = mixed + taps[k:k + 1, cols] * jnp.where(row >= k, pltpu.roll(values, k, 0), 0.0)
        sig_mix = jax.nn.sigmoid(mixed)
        act = mixed * sig_mix
        hidden[:, cols] = (act * gate).astype(BF16)
        gate_slope = act * gate * (1.0 - gate)
        mix_slope = gate * sig_mix * (1.0 + mixed * (1.0 - sig_mix))
        for m, out in enumerate((mine, other)):
            out[:length, cols] = gate_slope[m * length:(m + 1) * length]
            out[length:2 * length, cols] = mix_slope[m * length:(m + 1) * length]
    for out in (mine, other):
        out[2 * length:2 * length + 4, :] = taps[...]
        for n in range(width // channels):
            out[2 * length + 4 + n:2 * length + 5 + n, :] = gain[:, n * channels:(n + 1) * channels]
    copies[2].wait()
    copies[3].wait()


def assemble(place, pieces, up, length):
    micro, share, _ = pieces[0].shape
    tp = len(pieces)
    for k in range(tp):
        at = lax.rem(place[0] - k + tp, tp)
        for m in range(micro):
            start = pl.multiple_of(m * length + at * share, share)
            up[pl.ds(start, share), :] = pieces[k][m]


def pick_kernel(length, block, place, upstream, keep, send, up):
    for n, at in enumerate((place[3], 1 - place[3])):
        up[n * length:(n + 1) * length, :] = upstream[at]
    pick_columns(up, keep, place[1], block)
    pick_columns(up, send, 1 - place[1], block)


def start_either(yes, first, second, target, sem):
    @pl.when(yes)
    def _():
        pltpu.make_async_copy(first, target, sem).start()

    @pl.when(jnp.logical_not(yes))
    def _():
        pltpu.make_async_copy(second, target, sem).start()

    return pltpu.make_async_copy(first, target, sem)


def fetch_kernel(which, place, *refs):
    number = (len(refs) - 1) // 3
    own, other, outs, sems = refs[:number], refs[number:2 * number], refs[2 * number:-1], refs[-1]
    copies = [start_either(place[3] == which, own[n], other[n], outs[n], sems.at[n]) for n in range(number)]
    for copy in copies:
        copy.wait()


def copy_kernel(place, *refs):
    number = (len(refs) - 1) // 2
    copies = [pltpu.make_async_copy(refs[n], refs[number + n], refs[-1].at[n]) for n in range(number)]
    for copy in copies:
        copy.start()
    for copy in copies:
        copy.wait()


def tick_kernel(whole, length, block, place, *refs):
    if whole:
        upstream, value_w, gate_w, out_w, *parcels, both, own, sent1, sent2, sent3, blocks, up, value_v, gate_v, out_v, sems = refs
        copies = [
            pltpu.make_async_copy(out_w, out_v, sems.at[2]),
            pltpu.make_async_copy(value_w, value_v, sems.at[0]),
            pltpu.make_async_copy(gate_w, gate_v, sems.at[1]),
        ]
        for n, at in enumerate((place[3], 1 - place[3])):
            copies.insert(0, pltpu.make_async_copy(upstream.at[at], up.at[n * length:(n + 1) * length, :], sems.at[3 + n]))
        for copy in copies:
            copy.start()
        for copy in copies[:3]:
            copy.wait()
        copies = copies[3:]
    else:
        *pieces, out_v, value_v, gate_v, parcel, joint, pair, own, sent1, sent2, sent3, blocks, up = refs
        parcels = [parcel]
        copies = []
        assemble(place, pieces, up, length)
        both, send = joint.at[:length, :], joint.at[length:, :]
    tp, micro, share, width = blocks.shape
    rows, channels = up.shape[0], both.shape[1] // 2
    for n in range(0, channels, CHUNK):
        cols = slice(n, n + CHUNK)
        slopes = [parcel[:, cols] for parcel in parcels]
        gate_slope = jnp.concatenate([slope[:length] for slope in slopes], axis=0)
        mix_slope = jnp.concatenate([slope[length:2 * length] for slope in slopes], axis=0)
        taps = [slopes[0][2 * length + k:2 * length + k + 1] for k in range(4)]
        d_hidden = dot(up[...], out_v[cols, :], ((1,), (1,)))
        both[:, channels + n:channels + n + CHUNK] = (d_hidden * gate_slope).astype(BF16)
        d_mixed = d_hidden * mix_slope
        row = row_in_sequence(d_mixed.shape, length)
        d_values = taps[0] * d_mixed
        for k in range(1, 4):
            d_values = d_values + taps[k] * jnp.where(row < length - k, pltpu.roll(d_mixed, rows - k, 0), 0.0)
        both[:, cols] = d_values.astype(BF16)
    for copy in copies:
        copy.wait()
    part = 2 * CHUNK
    for n in range(0, width, part):
        cols = slice(n, n + part)
        d_normed = dot(both[:, :channels], value_v[cols, :], ((1,), (1,))) + dot(both[:, channels:], gate_v[cols, :], ((1,), (1,)))
        d_normed = d_normed.astype(BF16).reshape(micro, tp, share, part)
        for j in range(tp):
            blocks[j, :, :, cols] = d_normed[:, j]
    for k, out in enumerate((own, sent1, sent2, sent3)):
        out[...] = blocks[lax.rem(place[0] + k, tp)]
    if not whole:
        pair[:length, :] = both[...]
        pick_columns(up, pair.at[length:, :], place[1], block)
        pick_columns(up, send, 1 - place[1], block)


def norm_kernel(length, place, own, got1, got2, got3, *refs):
    micro, share, width = own.shape
    channels = refs[0].shape[1]
    parts = width // channels
    for m in range(micro):
        parcel, upstream, out = refs[m], refs[micro + m], refs[2 * micro + m]
        start = 2 * length + 4
        gain = jnp.concatenate([parcel[start + n:start + n + 1, :] for n in range(parts)], axis=1)
        start += parts
        x = jnp.concatenate([parcel[start + n * share:start + (n + 1) * share, :] for n in range(parts)], axis=1)
        inv_rms = lax.rsqrt(jnp.mean(x * x, axis=-1, keepdims=True) + EPSILON)
        unit = x * inv_rms
        d_unit = own[m].astype(F32) + got1[m].astype(F32) + got2[m].astype(F32) + got3[m].astype(F32)
        d_unit = d_unit * gain
        mean = jnp.mean(d_unit * unit, axis=-1, keepdims=True)
        out[0] = (upstream[0].astype(F32) + inv_rms * (d_unit - unit * mean)).astype(BF16)


def load_factors(place, refs, both, keep, send, n_got, hidden_got, sems):
    length = keep.shape[0] // 2
    top, bottom = pl.ds(0, length), pl.ds(length, length)
    moves = [(4, None, n_got), (5, None, hidden_got)]
    for n in range(4):
        moves.append((n, top, both.at[pl.ds(n * length, length), :]))
        moves.append((n, bottom, (keep if n < 2 else send).at[pl.ds(n % 2 * length, length), :]))
    for option in range(3):
        @pl.when(place[4] == option)
        def _():
            for at, (n, rows, target) in enumerate(moves):
                source = refs[3 * n + option]
                pltpu.make_async_copy(source if rows is None else source.at[rows, :], target, sems.at[at]).start()
    for at, (n, rows, target) in enumerate(moves):
        pltpu.make_async_copy(refs[3 * n] if rows is None else refs[3 * n].at[rows, :], target, sems.at[at]).wait()


def first_kernel(place, n_keep, hidden, *refs):
    refs, (forward, backward, both, keep, send, n_got, hidden_got, sems) = refs[:18], refs[18:]
    load_factors(place, refs, both, keep, send, n_got, hidden_got, sems)
    block = forward.shape[0]
    layers, (rows, channels) = n_keep.shape[1] // block, hidden.shape
    for ahead, out in ((layers // 2, forward), (layers // 2 + 1, backward)):
        some = pl.ds(pl.multiple_of(lax.rem(place[2] + ahead, layers) * block, block), block)
        n_sum = dot(n_keep[:, some].T, both[:rows, :], ((1,), (0,))) + dot(n_got[:, some].T, both[rows:, :], ((1,), (0,)))
        u_sum = dot(keep[:, some].T, hidden[...], ((1,), (0,))) + dot(send[:, some].T, hidden_got[...], ((1,), (0,)))
        out[:, :2 * channels] = n_sum.astype(BF16)
        out[:, 2 * channels:] = u_sum.astype(BF16)


def grads_kernel(place, n_keep, hidden, *refs):
    refs, (parts, left, both, keep, send, n_got, hidden_got, sems) = refs[:18], refs[18:]
    load_factors(place, refs, both, keep, send, n_got, hidden_got, sems)
    layers, block, _ = parts.shape
    rows, channels = hidden.shape

    def products(right, columns, base):
        def some(n):
            start = pl.multiple_of(n * CHUNK, CHUNK)
            out = dot(left[...], right[:, pl.ds(start, CHUNK)], ((1,), (0,)))
            parts[:, :, pl.ds(pl.multiple_of(base + start, CHUNK), CHUNK)] = out.astype(BF16).reshape(layers, block, CHUNK)

        steps(columns // CHUNK, some, False)

    left[:, :rows] = n_keep[...].T
    left[:, rows:] = n_got[...].T
    products(both, 2 * channels, 0)
    left[:, :rows] = keep[...].T
    left[:, rows:] = send[...].T
    both[:rows, :channels] = hidden[...]
    both[rows:, :channels] = hidden_got[...]
    products(both, channels, 2 * channels)


def ring_kernel(ahead, place, arrived, parts, out):
    layers = parts.shape[0]
    at = lax.rem(place[2] + ahead + layers, layers)
    out[...] = (arrived[...].astype(F32) + parts[at].astype(F32)).astype(BF16)


def close_kernel(factor, place, forward, backward, parts, value, gate, out):
    total = (parts[place[2]].astype(F32) + forward[...].astype(F32) + backward[...].astype(F32)) * factor
    channels = value.shape[1]
    value[...] = total[:, :channels]
    gate[...] = total[:, channels:2 * channels]
    out[...] = total[:, 2 * channels:]


def shards(activations, upstream_grad, norm_gain, value_weight, gate_weight, out_weight, conv_weight):
    acts, taps = activations[0], conv_weight[0]
    value_w, gate_w, out_w = value_weight[0], gate_weight[0], out_weight[0]
    sections, section = lax.axis_size("pp"), lax.axis_index("pp")
    tp, tp_index = lax.axis_size("tp"), lax.axis_index("tp")
    dp, dp_index = lax.axis_size("dp"), lax.axis_index("dp")
    micro, length, width = acts.shape
    channels = value_w.shape[1]
    rows, share, block = micro * length, length // tp, width // dp
    layers = dp // 2
    half = layers * block
    last = sections - 1
    factor = (rows * dp) ** (-0.5)
    core = section % 2

    place = jnp.stack([tp_index, dp_index % 2, dp_index // 2, core, jnp.where(section < 2, 2 - section, 0)]).astype(jnp.int32)

    def across(a):
        return lax.ppermute(a, "dp", [(i, i ^ 1) for i in range(dp)])

    def along(a, by):
        return lax.ppermute(a, "dp", [(i, (i + 2 * by) % dp) for i in range(dp)])

    def around(a, by):
        return lax.ppermute(a, "tp", [(i, (i + by) % tp) for i in range(tp)])

    def swap(a, flip):
        return lax.ppermute(a, "pp", [(p, p ^ flip) for p in range(sections)])

    def after(a, first):
        return lax.optimization_barrier((a, first))[0]

    piece, wide = shape((1, share, width), BF16), shape((micro, share, width), BF16)
    tokens, side = shape((rows, channels), BF16), shape((rows, half), BF16)
    joint = shape((2 * length, 2 * channels), BF16)
    parcel = shape((2 * length + 4 + width // channels * (1 + share), channels), F32)
    weight = pltpu.VMEM((width, channels), BF16)
    out_weight_v = pltpu.VMEM((channels, width), BF16)
    everything, everything_half = pltpu.VMEM((rows, width), BF16), pltpu.VMEM((length, width), BF16)

    def lent(a):
        pairs = [(p, p ^ 1) for p in range(sections) if p != last]
        return lax.ppermute(a, "pp", pairs)

    value_o, gate_o, out_o = lent(value_w), lent(gate_w), lent(out_w)
    mine, other, hidden, n_keep, n_send, up_mine, up_other = in_vmem(
        functools.partial(forward_kernel, block),
        [parcel, parcel, tokens, side, side, piece, piece],
        [everything, weight, weight, pltpu.VMEM(acts.shape, BF16), pltpu.VMEM(norm_gain.shape, F32), pltpu.VMEM(taps.shape, F32), pltpu.SemaphoreType.DMA((8,))],
        place, acts, norm_gain, taps, upstream_grad, value_w, gate_w, left_out=range(6), mib=24,
    )

    def scattered(sent):
        far = around(sent[1], 2)
        return [around(sent[0], 1), far, around(sent[2], 3)]

    def gathered(arrived):
        far = around(arrived, 2)
        return [arrived, around(arrived, 1), far, around(arrived, 3)]

    def untouched(*shapes):
        return pl.pallas_call(
            lambda *refs: None, out_shape=[shape(a.shape, a.dtype) for a in shapes], out_specs=[pl.BlockSpec(memory_space=pl.ANY)] * len(shapes),
        )()

    def copied(*arrays):
        return in_vmem(
            copy_kernel, [shape(a.shape, a.dtype) for a in arrays], [pltpu.SemaphoreType.DMA((len(arrays),))],
            place, *arrays, left_out=range(len(arrays)), mib=8,
        )

    def fetched(which, parcel_o):
        a, b = (out_w, value_w, gate_w, mine), (out_o, value_o, gate_o, parcel_o)
        return in_vmem(
            functools.partial(fetch_kernel, which), [shape(x.shape, x.dtype) for x in a], [pltpu.SemaphoreType.DMA((len(a),))],
            place, *a, *b, left_out=range(2 * len(a)), mib=12,
        )

    def linear(here, pieces):
        return in_vmem(
            functools.partial(tick_kernel, False, length, block), [joint, joint] + [piece] * 4,
            [pltpu.VMEM((tp,) + piece.shape, BF16), everything_half], place, *pieces, *here, mib=16,
        )

    def summed(here, upstream, own, got):
        return in_vmem(functools.partial(norm_kernel, length), [piece], [], place, own, *got, here[3], upstream)[0]

    def early():
        return across(n_send), across(hidden)

    both_whole = shape((rows, 2 * channels), BF16)

    def opening():
        def begin():
            both_3, own, *sent = in_vmem(
                functools.partial(tick_kernel, True, length, block), [both_whole] + [wide] * 4,
                [pltpu.VMEM((tp,) + wide.shape, BF16), everything, weight, weight, out_weight_v, pltpu.SemaphoreType.DMA((5,))],
                place, upstream_grad, value_w, gate_w, out_w, mine, other, left_out=(0, 1, 2, 3), mib=28,
            )
            return *in_vmem(
                functools.partial(norm_kernel, length), [piece] * 2, [], place, own, *scattered(sent), mine, other, up_mine, up_other
            ), both_3

        parcel_o = lent(other)
        share_3, share_3o, both_3 = lax.cond(section == last, begin, lambda: untouched(piece, piece, both_whole))
        arrived = jnp.where(core == 1, share_3, swap(share_3o, 1))
        pieces, here = gathered(arrived), fetched(0, parcel_o)
        joint_2, pair_2, own, *sent = linear(here, pieces)
        share_2 = summed(here, arrived, own, scattered(sent))
        return share_2, joint_2, pair_2, share_3, share_3o, both_3, *untouched(parcel, side, tokens)

    def waiting():
        return *untouched(piece, joint, joint, piece, piece, both_whole), lent(other), *early()

    share_2, joint_2, pair_2, share_3, share_3o, both_3, parcel_o, n_got, h_got = lax.cond(section < 2, waiting, opening)
    arrived = swap(share_2, 2)

    def closing(arrived, *_):
        pieces, here = gathered(arrived), fetched(1, parcel_o)
        joint_1, pair_1, own, *sent = linear(here, pieces)
        got = scattered(sent)
        next_here = fetched(0, after(parcel_o, own))
        share_1 = summed(here, arrived, own, after(got, next_here[0]))
        here, pieces = next_here, gathered(share_1)
        joint_1x = across(after(joint_1, share_1))
        pair_1o = swap(after(pair_1, share_1), 1)
        joint_0, pair_0, own, *sent = linear(here, after(pieces, pair_1o))
        joint_0x = across(joint_0)
        got = scattered(sent)
        pair_0o = swap(pair_0, 1)
        share_0 = summed(here, share_1, own, got)
        joint_1o, joint_0o = swap(after(joint_1x, share_0), 1), swap(joint_0x, 1)
        out = []
        for first, second in ((pair_1, pair_0), (pair_1o, pair_0o), (joint_1x, joint_0x), (joint_1o, joint_0o)):
            out += [untouched(joint)[0], first, second]
        return (*out, *untouched(side, tokens), jnp.where(core == 0, share_0, share_1), jnp.where(core == 0, share_1, share_0))

    def hand_over(arrived, share_2, joint_2, pair_2, share_3, share_3o, both_3):
        keep_3, send_3 = in_vmem(functools.partial(pick_kernel, length, block), [side, side], [everything], place, upstream_grad)

        def chosen(whole, rows, half):
            return jnp.where(core == 1, jnp.concatenate([both_3[rows], whole[rows]], axis=0), half)

        mine, other = slice(0, length), slice(length, rows)
        pair_m, pair_o = chosen(keep_3, mine, pair_2), chosen(keep_3, other, swap(pair_2, 1))
        joint_m, joint_o = chosen(send_3, mine, joint_2), chosen(send_3, other, swap(joint_2, 1))
        out = []
        for only in (pair_m, pair_o, across(joint_m), across(joint_o)):
            out += [only, *untouched(joint, joint)]
        return (*out, *early(), jnp.where(core == 1, share_3, share_2), share_2)

    *choices, n_far, h_far, share_m, share_o = lax.cond(
        section < 2, closing, hand_over, arrived, share_2, joint_2, pair_2, share_3, share_3o, both_3
    )
    share_o = swap(share_o, 1)
    share_o = jnp.where(section == last, share_3o, share_o)
    d_share = jnp.concatenate([jnp.where(core == 0, share_m, share_o), jnp.where(core == 0, share_o, share_m)], axis=0)
    factors = (n_keep, hidden, *choices, n_far, n_got, n_got, h_far, h_got, h_got)
    loaded = [
        pltpu.VMEM((2 * rows, 2 * channels), BF16), pltpu.VMEM(side.shape, BF16), pltpu.VMEM(side.shape, BF16),
        pltpu.VMEM(side.shape, BF16), pltpu.VMEM(tokens.shape, BF16), pltpu.SemaphoreType.DMA((10,)),
    ]
    moving = shape((block, 3 * channels), BF16)
    forward, backward = in_vmem(first_kernel, [moving] * 2, loaded, place, *factors, left_out=range(2, 20), mib=12)
    parts, = in_vmem(
        grads_kernel, [shape((layers, block, 3 * channels), BF16)], [pltpu.VMEM((half, 2 * rows), BF16)] + loaded,
        place, *after(factors, forward), left_out=range(2, 20), mib=16,
    )
    far, near = layers // 2, layers - 1 - layers // 2
    for step in range(far):
        forward = along(forward, 1)
        if step < far - 1:
            forward = in_vmem(functools.partial(ring_kernel, far - 1 - step), [moving], [], place, forward, parts)[0]
        if step < near:
            backward = along(backward, -1)
        if step < near - 1:
            backward = in_vmem(functools.partial(ring_kernel, step + 1 - near), [moving], [], place, backward, parts)[0]
    grads = in_vmem(
        functools.partial(close_kernel, factor), [shape((block, channels), F32)] * 3, [], place, forward, backward, parts,
    )
    return (d_share[None],) + tuple(g[None] for g in grads)


def solution(mesh):
    placed = (
        P("pp", None, "dp", None), P(None, "dp", None), P("pp", None), P("pp", None, "tp"),
        P("pp", None, "tp"), P("pp", "tp", None), P("pp", None, "tp"),
    )
    return jax.shard_map(
        shards, mesh=mesh, in_specs=placed,
        out_specs=(P("pp", None, ("dp", "tp"), None), P("pp", "dp", "tp"), P("pp", "dp", "tp"), P("pp", "dp", "tp")),
        check_vma=False,
    )
```

```python
import functools

import jax
import jax.numpy as jnp
from jax import lax
from jax.experimental import pallas as pl
from jax.experimental.pallas import tpu as pltpu
from jax.sharding import PartitionSpec as P

EPSILON = 1e-06
F32 = jnp.float32
BF16 = jnp.bfloat16
CHUNK = 256
BIG = 52


def dot(a, b, dims):
    return lax.dot_general(a, b, (dims, ((), ())), preferred_element_type=F32)


def in_vmem(kernel, outs, scratch, place, *operands, left_out=(), mib=8):
    whole, where_it_is = pl.BlockSpec(memory_space=pltpu.VMEM), pl.BlockSpec(memory_space=pltpu.HBM)
    return pl.pallas_call(
        kernel,
        out_shape=outs,
        in_specs=[pl.BlockSpec(memory_space=pltpu.SMEM)] + [where_it_is if n in left_out else whole for n in range(len(operands))],
        out_specs=[whole] * len(outs),
        scratch_shapes=scratch,
        compiler_params=pltpu.CompilerParams(vmem_limit_bytes=mib * 2**20),
    )(place, *operands)


def shape(dims, dtype):
    return jax.ShapeDtypeStruct(dims, dtype)


def row_in_sequence(dims, length):
    return lax.rem(lax.broadcasted_iota(jnp.int32, dims, 0), length)


def pick_columns(source, target, which, block):
    for layer in range(target.shape[1] // block):
        start = pl.multiple_of((2 * layer + which) * block, block)
        target[:, layer * block:(layer + 1) * block] = source[:, pl.ds(start, block)]


def steps(count, body, unroll=True):
    lax.fori_loop(0, count, lambda i, c: (body(i), c)[1], 0, unroll=unroll)


def forward_kernel(block, place, acts_at, gain_at, taps_at, upstream, value_w, gate_w, mine, other, hidden, keep, send, up_mine, up_other, normed, value_v, gate_v, acts, gain, taps, sems):
    micro, length, width = acts.shape
    share, channels = up_mine.shape[1], mine.shape[1]
    start = pl.multiple_of(place[0] * share, share)
    order = (place[3], 1 - place[3])
    first = [
        pltpu.make_async_copy(gain_at, gain, sems.at[4]),
        pltpu.make_async_copy(acts_at.at[order[0]], acts.at[0], sems.at[5]),
        pltpu.make_async_copy(acts_at.at[order[1]], acts.at[1], sems.at[6]),
        pltpu.make_async_copy(taps_at, taps, sems.at[7]),
    ]
    copies = [
        pltpu.make_async_copy(value_w, value_v, sems.at[0]),
        pltpu.make_async_copy(gate_w, gate_v, sems.at[1]),
        pltpu.make_async_copy(upstream.at[order[0], pl.ds(start, share), :], up_mine.at[0], sems.at[2]),
        pltpu.make_async_copy(upstream.at[order[1], pl.ds(start, share), :], up_other.at[0], sems.at[3]),
    ]
    for copy in first + copies:
        copy.start()
    first[0].wait()
    for n, out in enumerate((mine, other)):
        first[1 + n].wait()
        x = acts[n].astype(F32)
        inv_rms = lax.rsqrt(jnp.mean(x * x, axis=-1, keepdims=True) + EPSILON)
        normed[n * length:(n + 1) * length, :] = (x * inv_rms * gain[...]).astype(BF16)
        own = acts[n, pl.ds(start, share), :].astype(F32)
        for k in range(width // channels):
            at = 2 * length + 4 + width // channels + k * share
            out[at:at + share, :] = own[:, k * channels:(k + 1) * channels]
    pick_columns(normed, keep, place[1], block)
    pick_columns(normed, send, 1 - place[1], block)
    for copy in copies[:2] + first[3:]:
        copy.wait()
    for n in range(0, channels, CHUNK):
        cols = slice(n, n + CHUNK)
        values = dot(normed[...], value_v[:, cols], ((1,), (0,)))
        gate = jax.nn.sigmoid(dot(normed[...], gate_v[:, cols], ((1,), (0,))))
        row = row_in_sequence(values.shape, length)
        mixed = taps[0:1, cols] * values
        for k in range(1, taps.shape[0]):
            mixed = mixed + taps[k:k + 1, cols] * jnp.where(row >= k, pltpu.roll(values, k, 0), 0.0)
        sig_mix = jax.nn.sigmoid(mixed)
        act = mixed * sig_mix
        hidden[:, cols] = (act * gate).astype(BF16)
        gate_slope = act * gate * (1.0 - gate)
        mix_slope = gate * sig_mix * (1.0 + mixed * (1.0 - sig_mix))
        for m, out in enumerate((mine, other)):
            out[:length, cols] = gate_slope[m * length:(m + 1) * length]
            out[length:2 * length, cols] = mix_slope[m * length:(m + 1) * length]
    for out in (mine, other):
        out[2 * length:2 * length + 4, :] = taps[...]
        for n in range(width // channels):
            out[2 * length + 4 + n:2 * length + 5 + n, :] = gain[:, n * channels:(n + 1) * channels]
    copies[2].wait()
    copies[3].wait()


def way(place):
    return 1 - 2 * place[3]


def assemble(place, pieces, up, length):
    micro, share, _ = pieces[0].shape
    tp = len(pieces)
    for k in range(tp):
        at = lax.rem(place[0] - k + tp, tp)
        for m in range(micro):
            start = pl.multiple_of(m * length + at * share, share)
            up[pl.ds(start, share), :] = pieces[k][m]


def pick_kernel(length, block, place, upstream, keep, send, up):
    for n, at in enumerate((place[3], 1 - place[3])):
        up[n * length:(n + 1) * length, :] = upstream[at]
    pick_columns(up, keep, place[1], block)
    pick_columns(up, send, 1 - place[1], block)


def start_either(yes, first, second, target, sem):
    @pl.when(yes)
    def _():
        pltpu.make_async_copy(first, target, sem).start()

    @pl.when(jnp.logical_not(yes))
    def _():
        pltpu.make_async_copy(second, target, sem).start()

    return pltpu.make_async_copy(first, target, sem)


def fetch_kernel(which, place, *refs):
    number = (len(refs) - 1) // 3
    own, other, outs, sems = refs[:number], refs[number:2 * number], refs[2 * number:-1], refs[-1]
    copies = [start_either(place[3] == which, own[n], other[n], outs[n], sems.at[n]) for n in range(number)]
    for copy in copies:
        copy.wait()


def copy_kernel(place, *refs):
    number = (len(refs) - 1) // 2
    copies = [pltpu.make_async_copy(refs[n], refs[number + n], refs[-1].at[n]) for n in range(number)]
    for copy in copies:
        copy.start()
    for copy in copies:
        copy.wait()


def tick_kernel(whole, length, block, place, *refs):
    if whole:
        upstream, value_w, gate_w, out_w, *parcels, both, own, sent1, sent2, sent3, blocks, up, value_v, gate_v, out_v, sems = refs
        copies = [
            pltpu.make_async_copy(out_w, out_v, sems.at[2]),
            pltpu.make_async_copy(value_w, value_v, sems.at[0]),
            pltpu.make_async_copy(gate_w, gate_v, sems.at[1]),
        ]
        for n, at in enumerate((place[3], 1 - place[3])):
            copies.insert(0, pltpu.make_async_copy(upstream.at[at], up.at[n * length:(n + 1) * length, :], sems.at[3 + n]))
        for copy in copies:
            copy.start()
        for copy in copies[:3]:
            copy.wait()
        copies = copies[3:]
    else:
        *pieces, out_v, value_v, gate_v, parcel, joint, pair, own, sent1, sent2, sent3, blocks, up = refs
        parcels = [parcel]
        copies = []
        assemble(place, pieces, up, length)
        both, send = joint.at[:length, :], joint.at[length:, :]
    tp, micro, share, width = blocks.shape
    rows, channels = up.shape[0], both.shape[1] // 2
    for n in range(0, channels, CHUNK):
        cols = slice(n, n + CHUNK)
        slopes = [parcel[:, cols] for parcel in parcels]
        gate_slope = jnp.concatenate([slope[:length] for slope in slopes], axis=0)
        mix_slope = jnp.concatenate([slope[length:2 * length] for slope in slopes], axis=0)
        taps = [slopes[0][2 * length + k:2 * length + k + 1] for k in range(4)]
        d_hidden = dot(up[...], out_v[cols, :], ((1,), (1,)))
        both[:, channels + n:channels + n + CHUNK] = (d_hidden * gate_slope).astype(BF16)
        d_mixed = d_hidden * mix_slope
        row = row_in_sequence(d_mixed.shape, length)
        d_values = taps[0] * d_mixed
        for k in range(1, 4):
            d_values = d_values + taps[k] * jnp.where(row < length - k, pltpu.roll(d_mixed, rows - k, 0), 0.0)
        both[:, cols] = d_values.astype(BF16)
    for copy in copies:
        copy.wait()
    part = 2 * CHUNK
    for n in range(0, width, part):
        cols = slice(n, n + part)
        d_normed = dot(both[:, :channels], value_v[cols, :], ((1,), (1,))) + dot(both[:, channels:], gate_v[cols, :], ((1,), (1,)))
        d_normed = d_normed.astype(BF16).reshape(micro, tp, share, part)
        for j in range(tp):
            blocks[j, :, :, cols] = d_normed[:, j]
    for k, out in enumerate((own, sent1, sent2, sent3)):
        out[...] = blocks[lax.rem(place[0] + k, tp)]
    if not whole:
        pair[:length, :] = both[...]
        pick_columns(up, pair.at[length:, :], place[1], block)
        pick_columns(up, send, 1 - place[1], block)


def norm_kernel(length, place, own, got1, got2, got3, *refs):
    micro, share, width = own.shape
    channels = refs[0].shape[1]
    parts = width // channels
    for m in range(micro):
        parcel, upstream, out = refs[m], refs[micro + m], refs[2 * micro + m]
        start = 2 * length + 4
        gain = jnp.concatenate([parcel[start + n:start + n + 1, :] for n in range(parts)], axis=1)
        start += parts
        x = jnp.concatenate([parcel[start + n * share:start + (n + 1) * share, :] for n in range(parts)], axis=1)
        inv_rms = lax.rsqrt(jnp.mean(x * x, axis=-1, keepdims=True) + EPSILON)
        unit = x * inv_rms
        d_unit = own[m].astype(F32) + got1[m].astype(F32) + got2[m].astype(F32) + got3[m].astype(F32)
        d_unit = d_unit * gain
        mean = jnp.mean(d_unit * unit, axis=-1, keepdims=True)
        out[0] = (upstream[0].astype(F32) + inv_rms * (d_unit - unit * mean)).astype(BF16)


def load_factors(place, refs, both, keep, send, n_got, hidden_got, sems):
    length = keep.shape[0] // 2
    top, bottom = pl.ds(0, length), pl.ds(length, length)
    moves = [(4, None, n_got), (5, None, hidden_got)]
    for n in range(4):
        moves.append((n, top, both.at[pl.ds(n * length, length), :]))
        moves.append((n, bottom, (keep if n < 2 else send).at[pl.ds(n % 2 * length, length), :]))
    for option in range(3):
        @pl.when(place[4] == option)
        def _():
            for at, (n, rows, target) in enumerate(moves):
                source = refs[3 * n + option]
                pltpu.make_async_copy(source if rows is None else source.at[rows, :], target, sems.at[at]).start()
    for at, (n, rows, target) in enumerate(moves):
        pltpu.make_async_copy(refs[3 * n] if rows is None else refs[3 * n].at[rows, :], target, sems.at[at]).wait()


def first_kernel(place, n_keep, hidden, *refs):
    refs, (forward, backward, both, keep, send, n_got, hidden_got, sems) = refs[:18], refs[18:]
    load_factors(place, refs, both, keep, send, n_got, hidden_got, sems)
    block = forward.shape[0]
    layers, (rows, channels) = n_keep.shape[1] // block, hidden.shape
    far = layers // 2
    for ahead, out in ((far, forward), (far + 1 - layers, backward)):
        some = pl.ds(pl.multiple_of(lax.rem(place[2] + way(place) * ahead + layers, layers) * block, block), block)
        n_sum = dot(n_keep[:, some].T, both[:rows, :], ((1,), (0,))) + dot(n_got[:, some].T, both[rows:, :], ((1,), (0,)))
        u_sum = dot(keep[:, some].T, hidden[...], ((1,), (0,))) + dot(send[:, some].T, hidden_got[...], ((1,), (0,)))
        out[:, :2 * channels] = n_sum.astype(BF16)
        out[:, 2 * channels:] = u_sum.astype(BF16)


def grads_kernel(place, n_keep, hidden, *refs):
    refs, (parts, left, both, keep, send, n_got, hidden_got, sems) = refs[:18], refs[18:]
    load_factors(place, refs, both, keep, send, n_got, hidden_got, sems)
    layers, block, _ = parts.shape
    rows, channels = hidden.shape

    def products(right, columns, base):
        def some(n):
            start = pl.multiple_of(n * CHUNK, CHUNK)
            out = dot(left[...], right[:, pl.ds(start, CHUNK)], ((1,), (0,)))
            parts[:, :, pl.ds(pl.multiple_of(base + start, CHUNK), CHUNK)] = out.astype(BF16).reshape(layers, block, CHUNK)

        steps(columns // CHUNK, some, False)

    left[:, :rows] = n_keep[...].T
    left[:, rows:] = n_got[...].T
    products(both, 2 * channels, 0)
    left[:, :rows] = keep[...].T
    left[:, rows:] = send[...].T
    both[:rows, :channels] = hidden[...]
    both[rows:, :channels] = hidden_got[...]
    products(both, channels, 2 * channels)


def ring_kernel(ahead, place, arrived, parts, out):
    layers = parts.shape[0]
    at = lax.rem(place[2] + way(place) * ahead + layers, layers)
    out[...] = (arrived[...].astype(F32) + parts[at].astype(F32)).astype(BF16)


def close_kernel(factor, place, forward, backward, parts, value, gate, out):
    total = (parts[place[2]].astype(F32) + forward[...].astype(F32) + backward[...].astype(F32)) * factor
    channels = value.shape[1]
    value[...] = total[:, :channels]
    gate[...] = total[:, channels:2 * channels]
    out[...] = total[:, 2 * channels:]


def shards(activations, upstream_grad, norm_gain, value_weight, gate_weight, out_weight, conv_weight):
    acts, taps = activations[0], conv_weight[0]
    value_w, gate_w, out_w = value_weight[0], gate_weight[0], out_weight[0]
    sections, section = lax.axis_size("pp"), lax.axis_index("pp")
    tp, tp_index = lax.axis_size("tp"), lax.axis_index("tp")
    dp, dp_index = lax.axis_size("dp"), lax.axis_index("dp")
    micro, length, width = acts.shape
    channels = value_w.shape[1]
    rows, share, block = micro * length, length // tp, width // dp
    layers = dp // 2
    half = layers * block
    last = sections - 1
    factor = (rows * dp) ** (-0.5)
    core = section % 2

    place = jnp.stack([tp_index, dp_index % 2, dp_index // 2, core, jnp.where(section < 2, 2 - section, 0)]).astype(jnp.int32)

    def across(a):
        return lax.ppermute(a, "dp", [(i, i ^ 1) for i in range(dp)])

    def along(a, by):
        pairs = [(p * dp + i, p * dp + (i + (2 if p % 2 == 0 else -2) * by) % dp) for p in range(sections) for i in range(dp)]
        return lax.ppermute(a, ("pp", "dp"), pairs)

    def around(a, by):
        return lax.ppermute(a, "tp", [(i, (i + by) % tp) for i in range(tp)])

    def swap(a, flip):
        return lax.ppermute(a, "pp", [(p, p ^ flip) for p in range(sections)])

    def after(a, first):
        return lax.optimization_barrier((a, first))[0]

    piece, wide = shape((1, share, width), BF16), shape((micro, share, width), BF16)
    tokens, side = shape((rows, channels), BF16), shape((rows, half), BF16)
    joint = shape((2 * length, 2 * channels), BF16)
    parcel = shape((2 * length + 4 + width // channels * (1 + share), channels), F32)
    weight = pltpu.VMEM((width, channels), BF16)
    out_weight_v = pltpu.VMEM((channels, width), BF16)
    everything, everything_half = pltpu.VMEM((rows, width), BF16), pltpu.VMEM((length, width), BF16)

    def lent(a):
        pairs = [(p, p ^ 1) for p in range(sections) if p != last]
        return lax.ppermute(a, "pp", pairs)

    value_o, gate_o, out_o = lent(value_w), lent(gate_w), lent(out_w)
    mine, other, hidden, n_keep, n_send, up_mine, up_other = in_vmem(
        functools.partial(forward_kernel, block),
        [parcel, parcel, tokens, side, side, piece, piece],
        [everything, weight, weight, pltpu.VMEM(acts.shape, BF16), pltpu.VMEM(norm_gain.shape, F32), pltpu.VMEM(taps.shape, F32), pltpu.SemaphoreType.DMA((8,))],
        place, acts, norm_gain, taps, upstream_grad, value_w, gate_w, left_out=range(6), mib=24,
    )

    def scattered(sent):
        far = around(sent[1], 2)
        return [around(sent[0], 1), far, around(sent[2], 3)]

    def gathered(arrived):
        far = around(arrived, 2)
        return [arrived, around(arrived, 1), far, around(arrived, 3)]

    def untouched(*shapes):
        return pl.pallas_call(
            lambda *refs: None, out_shape=[shape(a.shape, a.dtype) for a in shapes], out_specs=[pl.BlockSpec(memory_space=pl.ANY)] * len(shapes),
        )()

    def copied(*arrays):
        return in_vmem(
            copy_kernel, [shape(a.shape, a.dtype) for a in arrays], [pltpu.SemaphoreType.DMA((len(arrays),))],
            place, *arrays, left_out=range(len(arrays)), mib=8,
        )

    def fetched(which, parcel_o):
        a, b = (out_w, value_w, gate_w, mine), (out_o, value_o, gate_o, parcel_o)
        return in_vmem(
            functools.partial(fetch_kernel, which), [shape(x.shape, x.dtype) for x in a], [pltpu.SemaphoreType.DMA((len(a),))],
            place, *a, *b, left_out=range(2 * len(a)), mib=12,
        )

    def linear(here, pieces):
        return in_vmem(
            functools.partial(tick_kernel, False, length, block), [joint, joint] + [piece] * 4,
            [pltpu.VMEM((tp,) + piece.shape, BF16), everything_half], place, *pieces, *here, mib=16,
        )

    def summed(here, upstream, own, got):
        return in_vmem(functools.partial(norm_kernel, length), [piece], [], place, own, *got, here[3], upstream)[0]

    def early():
        return across(n_send), across(hidden)

    both_whole = shape((rows, 2 * channels), BF16)

    def opening():
        def begin():
            both_3, own, *sent = in_vmem(
                functools.partial(tick_kernel, True, length, block), [both_whole] + [wide] * 4,
                [pltpu.VMEM((tp,) + wide.shape, BF16), everything, weight, weight, out_weight_v, pltpu.SemaphoreType.DMA((5,))],
                place, upstream_grad, value_w, gate_w, out_w, mine, other, left_out=(0, 1, 2, 3), mib=28,
            )
            return *in_vmem(
                functools.partial(norm_kernel, length), [piece] * 2, [], place, own, *scattered(sent), mine, other, up_mine, up_other
            ), both_3

        parcel_o = lent(other)
        share_3, share_3o, both_3 = lax.cond(section == last, begin, lambda: untouched(piece, piece, both_whole))
        arrived = jnp.where(core == 1, share_3, swap(share_3o, 1))
        pieces, here = gathered(arrived), fetched(0, parcel_o)
        joint_2, pair_2, own, *sent = linear(here, pieces)
        share_2 = summed(here, arrived, own, scattered(sent))
        return share_2, joint_2, pair_2, share_3, share_3o, both_3, *untouched(parcel, side, tokens)

    def waiting():
        return *untouched(piece, joint, joint, piece, piece, both_whole), lent(other), *early()

    share_2, joint_2, pair_2, share_3, share_3o, both_3, parcel_o, n_got, h_got = lax.cond(section < 2, waiting, opening)
    arrived = swap(share_2, 2)

    def closing(arrived, *_):
        pieces, here = gathered(arrived), fetched(1, parcel_o)
        joint_1, pair_1, own, *sent = linear(here, pieces)
        got = scattered(sent)
        next_here = fetched(0, after(parcel_o, own))
        share_1 = summed(here, arrived, own, after(got, next_here[0]))
        here, pieces = next_here, gathered(share_1)
        joint_1x = across(after(joint_1, share_1))
        pair_1o = swap(after(pair_1, share_1), 1)
        joint_0, pair_0, own, *sent = linear(here, after(pieces, pair_1o))
        joint_0x = across(joint_0)
        got = scattered(sent)
        pair_0o = swap(pair_0, 1)
        share_0 = summed(here, share_1, own, got)
        joint_1o, joint_0o = swap(after(joint_1x, share_0), 1), swap(joint_0x, 1)
        out = []
        for first, second in ((pair_1, pair_0), (pair_1o, pair_0o), (joint_1x, joint_0x), (joint_1o, joint_0o)):
            out += [untouched(joint)[0], first, second]
        return (*out, *untouched(side, tokens), jnp.where(core == 0, share_0, share_1), jnp.where(core == 0, share_1, share_0))

    def hand_over(arrived, share_2, joint_2, pair_2, share_3, share_3o, both_3):
        keep_3, send_3 = in_vmem(functools.partial(pick_kernel, length, block), [side, side], [everything], place, upstream_grad)

        def chosen(whole, rows, half):
            return jnp.where(core == 1, jnp.concatenate([both_3[rows], whole[rows]], axis=0), half)

        mine, other = slice(0, length), slice(length, rows)
        pair_m, pair_o = chosen(keep_3, mine, pair_2), chosen(keep_3, other, swap(pair_2, 1))
        joint_m, joint_o = chosen(send_3, mine, joint_2), chosen(send_3, other, swap(joint_2, 1))
        out = []
        for only in (pair_m, pair_o, across(joint_m), across(joint_o)):
            out += [only, *untouched(joint, joint)]
        return (*out, *early(), jnp.where(core == 1, share_3, share_2), share_2)

    *choices, n_far, h_far, share_m, share_o = lax.cond(
        section < 2, closing, hand_over, arrived, share_2, joint_2, pair_2, share_3, share_3o, both_3
    )
    share_o = swap(share_o, 1)
    share_o = jnp.where(section == last, share_3o, share_o)
    d_share = jnp.concatenate([jnp.where(core == 0, share_m, share_o), jnp.where(core == 0, share_o, share_m)], axis=0)
    factors = (n_keep, hidden, *choices, n_far, n_got, n_got, h_far, h_got, h_got)
    loaded = [
        pltpu.VMEM((2 * rows, 2 * channels), BF16), pltpu.VMEM(side.shape, BF16), pltpu.VMEM(side.shape, BF16),
        pltpu.VMEM(side.shape, BF16), pltpu.VMEM(tokens.shape, BF16), pltpu.SemaphoreType.DMA((10,)),
    ]
    moving = shape((block, 3 * channels), BF16)
    forward, backward = in_vmem(first_kernel, [moving] * 2, loaded, place, *factors, left_out=range(2, 20), mib=12)
    parts, = in_vmem(
        grads_kernel, [shape((layers, block, 3 * channels), BF16)], [pltpu.VMEM((half, 2 * rows), BF16)] + loaded,
        place, *after(factors, forward), left_out=range(2, 20), mib=16,
    )
    backward = after(backward, parts)
    far, near = layers // 2, layers - 1 - layers // 2
    for step in range(far):
        forward = along(forward, 1)
        if step < far - 1:
            forward = in_vmem(functools.partial(ring_kernel, far - 1 - step), [moving], [], place, forward, parts)[0]
        if step < near:
            backward = along(backward, -1)
        if step < near - 1:
            backward = in_vmem(functools.partial(ring_kernel, step + 1 - near), [moving], [], place, backward, parts)[0]
    grads = in_vmem(
        functools.partial(close_kernel, factor), [shape((block, channels), F32)] * 3, [], place, forward, backward, parts,
    )
    return (d_share[None],) + tuple(g[None] for g in grads)


def solution(mesh):
    placed = (
        P("pp", None, "dp", None), P(None, "dp", None), P("pp", None), P("pp", None, "tp"),
        P("pp", None, "tp"), P("pp", "tp", None), P("pp", None, "tp"),
    )
    return jax.shard_map(
        shards, mesh=mesh, in_specs=placed,
        out_specs=(P("pp", None, ("dp", "tp"), None), P("pp", "dp", "tp"), P("pp", "dp", "tp"), P("pp", "dp", "tp")),
        check_vma=False,
    )
```

```python
import functools

import jax
import jax.numpy as jnp
from jax import lax
from jax.experimental import pallas as pl
from jax.experimental.pallas import tpu as pltpu
from jax.sharding import PartitionSpec as P

EPSILON = 1e-06
F32 = jnp.float32
BF16 = jnp.bfloat16
CHUNK = 256
BIG = 52


def dot(a, b, dims):
    return lax.dot_general(a, b, (dims, ((), ())), preferred_element_type=F32)


def in_vmem(kernel, outs, scratch, place, *operands, left_out=(), mib=8):
    whole, where_it_is = pl.BlockSpec(memory_space=pltpu.VMEM), pl.BlockSpec(memory_space=pltpu.HBM)
    return pl.pallas_call(
        kernel,
        out_shape=outs,
        in_specs=[pl.BlockSpec(memory_space=pltpu.SMEM)] + [where_it_is if n in left_out else whole for n in range(len(operands))],
        out_specs=[whole] * len(outs),
        scratch_shapes=scratch,
        compiler_params=pltpu.CompilerParams(vmem_limit_bytes=mib * 2**20),
    )(place, *operands)


def shape(dims, dtype):
    return jax.ShapeDtypeStruct(dims, dtype)


def row_in_sequence(dims, length):
    return lax.rem(lax.broadcasted_iota(jnp.int32, dims, 0), length)


def pick_columns(source, target, which, block):
    for layer in range(target.shape[1] // block):
        start = pl.multiple_of((2 * layer + which) * block, block)
        target[:, layer * block:(layer + 1) * block] = source[:, pl.ds(start, block)]


def steps(count, body, unroll=True):
    lax.fori_loop(0, count, lambda i, c: (body(i), c)[1], 0, unroll=unroll)


def forward_kernel(block, place, acts_at, gain_at, taps_at, upstream, value_w, gate_w, mine, other, hidden, keep, send, up_mine, up_other, normed, value_v, gate_v, acts, gain, taps, sems):
    micro, length, width = acts.shape
    share, channels = up_mine.shape[1], mine.shape[1]
    start = pl.multiple_of(place[0] * share, share)
    order = (place[3], 1 - place[3])
    first = [
        pltpu.make_async_copy(gain_at, gain, sems.at[4]),
        pltpu.make_async_copy(acts_at.at[order[0]], acts.at[0], sems.at[5]),
        pltpu.make_async_copy(acts_at.at[order[1]], acts.at[1], sems.at[6]),
        pltpu.make_async_copy(taps_at, taps, sems.at[7]),
    ]
    copies = [
        pltpu.make_async_copy(value_w, value_v, sems.at[0]),
        pltpu.make_async_copy(gate_w, gate_v, sems.at[1]),
        pltpu.make_async_copy(upstream.at[order[0], pl.ds(start, share), :], up_mine.at[0], sems.at[2]),
        pltpu.make_async_copy(upstream.at[order[1], pl.ds(start, share), :], up_other.at[0], sems.at[3]),
    ]
    for copy in first + copies:
        copy.start()
    first[0].wait()
    for n, out in enumerate((mine, other)):
        first[1 + n].wait()
        x = acts[n].astype(F32)
        inv_rms = lax.rsqrt(jnp.mean(x * x, axis=-1, keepdims=True) + EPSILON)
        normed[n * length:(n + 1) * length, :] = (x * inv_rms * gain[...]).astype(BF16)
        own = acts[n, pl.ds(start, share), :].astype(F32)
        for k in range(width // channels):
            at = 2 * length + 4 + width // channels + k * share
            out[at:at + share, :] = own[:, k * channels:(k + 1) * channels]
    pick_columns(normed, keep, place[1], block)
    pick_columns(normed, send, 1 - place[1], block)
    for copy in copies[:2] + first[3:]:
        copy.wait()
    def columns(n):
        cols = pl.ds(pl.multiple_of(n * CHUNK, CHUNK), CHUNK)
        values = dot(normed[...], value_v[:, cols], ((1,), (0,)))
        gate = jax.nn.sigmoid(dot(normed[...], gate_v[:, cols], ((1,), (0,))))
        row = row_in_sequence(values.shape, length)
        mixed = taps[0:1, cols] * values
        for k in range(1, taps.shape[0]):
            mixed = mixed + taps[k:k + 1, cols] * jnp.where(row >= k, pltpu.roll(values, k, 0), 0.0)
        sig_mix = jax.nn.sigmoid(mixed)
        act = mixed * sig_mix
        hidden[:, cols] = (act * gate).astype(BF16)
        gate_slope = act * gate * (1.0 - gate)
        mix_slope = gate * sig_mix * (1.0 + mixed * (1.0 - sig_mix))
        for m, out in enumerate((mine, other)):
            out[:length, cols] = gate_slope[m * length:(m + 1) * length]
            out[length:2 * length, cols] = mix_slope[m * length:(m + 1) * length]
    steps(channels // CHUNK, columns, False)
    for out in (mine, other):
        out[2 * length:2 * length + 4, :] = taps[...]
        for n in range(width // channels):
            out[2 * length + 4 + n:2 * length + 5 + n, :] = gain[:, n * channels:(n + 1) * channels]
    copies[2].wait()
    copies[3].wait()


def way(place):
    return 1 - 2 * place[3]


def assemble(place, pieces, up, length):
    micro, share, _ = pieces[0].shape
    tp = len(pieces)
    for k in range(tp):
        at = lax.rem(place[0] - k + tp, tp)
        for m in range(micro):
            start = pl.multiple_of(m * length + at * share, share)
            up[pl.ds(start, share), :] = pieces[k][m]


def pick_kernel(length, block, place, upstream, keep, send, up):
    for n, at in enumerate((place[3], 1 - place[3])):
        up[n * length:(n + 1) * length, :] = upstream[at]
    pick_columns(up, keep, place[1], block)
    pick_columns(up, send, 1 - place[1], block)


def start_either(yes, first, second, target, sem):
    @pl.when(yes)
    def _():
        pltpu.make_async_copy(first, target, sem).start()

    @pl.when(jnp.logical_not(yes))
    def _():
        pltpu.make_async_copy(second, target, sem).start()

    return pltpu.make_async_copy(first, target, sem)


def fetch_kernel(which, place, *refs):
    number = (len(refs) - 1) // 3
    own, other, outs, sems = refs[:number], refs[number:2 * number], refs[2 * number:-1], refs[-1]
    copies = [start_either(place[3] == which, own[n], other[n], outs[n], sems.at[n]) for n in range(number)]
    for copy in copies:
        copy.wait()


def copy_kernel(place, *refs):
    number = (len(refs) - 1) // 2
    copies = [pltpu.make_async_copy(refs[n], refs[number + n], refs[-1].at[n]) for n in range(number)]
    for copy in copies:
        copy.start()
    for copy in copies:
        copy.wait()


def tick_kernel(whole, length, block, place, *refs):
    if whole:
        upstream, value_w, gate_w, out_w, *parcels, both, own, sent1, sent2, sent3, blocks, up, value_v, gate_v, out_v, sems = refs
        copies = [
            pltpu.make_async_copy(out_w, out_v, sems.at[2]),
            pltpu.make_async_copy(value_w, value_v, sems.at[0]),
            pltpu.make_async_copy(gate_w, gate_v, sems.at[1]),
        ]
        for n, at in enumerate((place[3], 1 - place[3])):
            copies.insert(0, pltpu.make_async_copy(upstream.at[at], up.at[n * length:(n + 1) * length, :], sems.at[3 + n]))
        for copy in copies:
            copy.start()
        for copy in copies[:3]:
            copy.wait()
        copies = copies[3:]
    else:
        *pieces, out_v, value_v, gate_v, parcel, joint, pair, own, sent1, sent2, sent3, blocks, up = refs
        parcels = [parcel]
        copies = []
        assemble(place, pieces, up, length)
        both, send = joint.at[:length, :], joint.at[length:, :]
    tp, micro, share, width = blocks.shape
    rows, channels = up.shape[0], both.shape[1] // 2
    def columns(n):
        start = pl.multiple_of(n * CHUNK, CHUNK)
        cols = pl.ds(start, CHUNK)
        slopes = [parcel[:, cols] for parcel in parcels]
        gate_slope = jnp.concatenate([slope[:length] for slope in slopes], axis=0)
        mix_slope = jnp.concatenate([slope[length:2 * length] for slope in slopes], axis=0)
        taps = [slopes[0][2 * length + k:2 * length + k + 1] for k in range(4)]
        d_hidden = dot(up[...], out_v[cols, :], ((1,), (1,)))
        both[:, pl.ds(pl.multiple_of(channels + start, CHUNK), CHUNK)] = (d_hidden * gate_slope).astype(BF16)
        d_mixed = d_hidden * mix_slope
        row = row_in_sequence(d_mixed.shape, length)
        d_values = taps[0] * d_mixed
        for k in range(1, 4):
            d_values = d_values + taps[k] * jnp.where(row < length - k, pltpu.roll(d_mixed, rows - k, 0), 0.0)
        both[:, cols] = d_values.astype(BF16)
    steps(channels // CHUNK, columns, False)
    for copy in copies:
        copy.wait()
    part = 2 * CHUNK
    def inputs(n):
        cols = pl.ds(pl.multiple_of(n * part, part), part)
        d_normed = dot(both[:, :channels], value_v[cols, :], ((1,), (1,))) + dot(both[:, channels:], gate_v[cols, :], ((1,), (1,)))
        d_normed = d_normed.astype(BF16).reshape(micro, tp, share, part)
        for j in range(tp):
            blocks[j, :, :, cols] = d_normed[:, j]
    steps(width // part, inputs, False)
    for k, out in enumerate((own, sent1, sent2, sent3)):
        out[...] = blocks[lax.rem(place[0] + k, tp)]
    if not whole:
        pair[:length, :] = both[...]
        pick_columns(up, pair.at[length:, :], place[1], block)
        pick_columns(up, send, 1 - place[1], block)


def norm_kernel(length, place, own, got1, got2, got3, *refs):
    micro, share, width = own.shape
    channels = refs[0].shape[1]
    parts = width // channels
    for m in range(micro):
        parcel, upstream, out = refs[m], refs[micro + m], refs[2 * micro + m]
        start = 2 * length + 4
        gain = jnp.concatenate([parcel[start + n:start + n + 1, :] for n in range(parts)], axis=1)
        start += parts
        x = jnp.concatenate([parcel[start + n * share:start + (n + 1) * share, :] for n in range(parts)], axis=1)
        inv_rms = lax.rsqrt(jnp.mean(x * x, axis=-1, keepdims=True) + EPSILON)
        unit = x * inv_rms
        d_unit = own[m].astype(F32) + got1[m].astype(F32) + got2[m].astype(F32) + got3[m].astype(F32)
        d_unit = d_unit * gain
        mean = jnp.mean(d_unit * unit, axis=-1, keepdims=True)
        out[0] = (upstream[0].astype(F32) + inv_rms * (d_unit - unit * mean)).astype(BF16)


def load_factors(place, refs, both, keep, send, n_got, hidden_got, sems):
    length = keep.shape[0] // 2
    top, bottom = pl.ds(0, length), pl.ds(length, length)
    moves = [(4, None, n_got), (5, None, hidden_got)]
    for n in range(4):
        moves.append((n, top, both.at[pl.ds(n * length, length), :]))
        moves.append((n, bottom, (keep if n < 2 else send).at[pl.ds(n % 2 * length, length), :]))
    for option in range(3):
        @pl.when(place[4] == option)
        def _():
            for at, (n, rows, target) in enumerate(moves):
                source = refs[3 * n + option]
                pltpu.make_async_copy(source if rows is None else source.at[rows, :], target, sems.at[at]).start()
    for at, (n, rows, target) in enumerate(moves):
        pltpu.make_async_copy(refs[3 * n] if rows is None else refs[3 * n].at[rows, :], target, sems.at[at]).wait()


def first_kernel(place, n_keep, hidden, *refs):
    refs, (forward, backward, both, keep, send, n_got, hidden_got, sems) = refs[:18], refs[18:]
    load_factors(place, refs, both, keep, send, n_got, hidden_got, sems)
    block = forward.shape[0]
    layers, (rows, channels) = n_keep.shape[1] // block, hidden.shape
    far = layers // 2
    for ahead, out in ((far, forward), (far + 1 - layers, backward)):
        some = pl.ds(pl.multiple_of(lax.rem(place[2] + way(place) * ahead + layers, layers) * block, block), block)
        n_sum = dot(n_keep[:, some].T, both[:rows, :], ((1,), (0,))) + dot(n_got[:, some].T, both[rows:, :], ((1,), (0,)))
        u_sum = dot(keep[:, some].T, hidden[...], ((1,), (0,))) + dot(send[:, some].T, hidden_got[...], ((1,), (0,)))
        out[:, :2 * channels] = n_sum.astype(BF16)
        out[:, 2 * channels:] = u_sum.astype(BF16)


def grads_kernel(place, n_keep, hidden, *refs):
    refs, (parts, left, both, keep, send, n_got, hidden_got, sems) = refs[:18], refs[18:]
    load_factors(place, refs, both, keep, send, n_got, hidden_got, sems)
    layers, block, _ = parts.shape
    rows, channels = hidden.shape

    def products(right, columns, base):
        def some(n):
            start = pl.multiple_of(n * CHUNK, CHUNK)
            out = dot(left[...], right[:, pl.ds(start, CHUNK)], ((1,), (0,)))
            parts[:, :, pl.ds(pl.multiple_of(base + start, CHUNK), CHUNK)] = out.astype(BF16).reshape(layers, block, CHUNK)

        steps(columns // CHUNK, some, False)

    left[:, :rows] = n_keep[...].T
    left[:, rows:] = n_got[...].T
    products(both, 2 * channels, 0)
    left[:, :rows] = keep[...].T
    left[:, rows:] = send[...].T
    both[:rows, :channels] = hidden[...]
    both[rows:, :channels] = hidden_got[...]
    products(both, channels, 2 * channels)


def ring_kernel(ahead, place, arrived, parts, out):
    layers = parts.shape[0]
    at = lax.rem(place[2] + way(place) * ahead + layers, layers)
    out[...] = (arrived[...].astype(F32) + parts[at].astype(F32)).astype(BF16)


def close_kernel(factor, place, forward, backward, parts, value, gate, out):
    total = (parts[place[2]].astype(F32) + forward[...].astype(F32) + backward[...].astype(F32)) * factor
    channels = value.shape[1]
    value[...] = total[:, :channels]
    gate[...] = total[:, channels:2 * channels]
    out[...] = total[:, 2 * channels:]


def shards(activations, upstream_grad, norm_gain, value_weight, gate_weight, out_weight, conv_weight):
    acts, taps = activations[0], conv_weight[0]
    value_w, gate_w, out_w = value_weight[0], gate_weight[0], out_weight[0]
    sections, section = lax.axis_size("pp"), lax.axis_index("pp")
    tp, tp_index = lax.axis_size("tp"), lax.axis_index("tp")
    dp, dp_index = lax.axis_size("dp"), lax.axis_index("dp")
    micro, length, width = acts.shape
    channels = value_w.shape[1]
    rows, share, block = micro * length, length // tp, width // dp
    layers = dp // 2
    half = layers * block
    last = sections - 1
    factor = (rows * dp) ** (-0.5)
    core = section % 2

    place = jnp.stack([tp_index, dp_index % 2, dp_index // 2, core, jnp.where(section < 2, 2 - section, 0)]).astype(jnp.int32)

    def across(a):
        return lax.ppermute(a, "dp", [(i, i ^ 1) for i in range(dp)])

    def along(a, by):
        pairs = [(p * dp + i, p * dp + (i + (2 if p % 2 == 0 else -2) * by) % dp) for p in range(sections) for i in range(dp)]
        return lax.ppermute(a, ("pp", "dp"), pairs)

    def around(a, by):
        return lax.ppermute(a, "tp", [(i, (i + by) % tp) for i in range(tp)])

    def swap(a, flip):
        return lax.ppermute(a, "pp", [(p, p ^ flip) for p in range(sections)])

    def after(a, first):
        return lax.optimization_barrier((a, first))[0]

    piece, wide = shape((1, share, width), BF16), shape((micro, share, width), BF16)
    tokens, side = shape((rows, channels), BF16), shape((rows, half), BF16)
    joint = shape((2 * length, 2 * channels), BF16)
    parcel = shape((2 * length + 4 + width // channels * (1 + share), channels), F32)
    weight = pltpu.VMEM((width, channels), BF16)
    out_weight_v = pltpu.VMEM((channels, width), BF16)
    everything, everything_half = pltpu.VMEM((rows, width), BF16), pltpu.VMEM((length, width), BF16)

    def lent(a):
        pairs = [(p, p ^ 1) for p in range(sections) if p != last]
        return lax.ppermute(a, "pp", pairs)

    value_o, gate_o, out_o = lent(value_w), lent(gate_w), lent(out_w)
    mine, other, hidden, n_keep, n_send, up_mine, up_other = in_vmem(
        functools.partial(forward_kernel, block),
        [parcel, parcel, tokens, side, side, piece, piece],
        [everything, weight, weight, pltpu.VMEM(acts.shape, BF16), pltpu.VMEM(norm_gain.shape, F32), pltpu.VMEM(taps.shape, F32), pltpu.SemaphoreType.DMA((8,))],
        place, acts, norm_gain, taps, upstream_grad, value_w, gate_w, left_out=range(6), mib=24,
    )

    def scattered(sent):
        far = around(sent[1], 2)
        return [around(sent[0], 1), far, around(sent[2], 3)]

    def gathered(arrived):
        far = around(arrived, 2)
        return [arrived, around(arrived, 1), far, around(arrived, 3)]

    def untouched(*shapes):
        return pl.pallas_call(
            lambda *refs: None, out_shape=[shape(a.shape, a.dtype) for a in shapes], out_specs=[pl.BlockSpec(memory_space=pl.ANY)] * len(shapes),
        )()

    def copied(*arrays):
        return in_vmem(
            copy_kernel, [shape(a.shape, a.dtype) for a in arrays], [pltpu.SemaphoreType.DMA((len(arrays),))],
            place, *arrays, left_out=range(len(arrays)), mib=8,
        )

    def fetched(which, parcel_o):
        a, b = (out_w, value_w, gate_w, mine), (out_o, value_o, gate_o, parcel_o)
        return in_vmem(
            functools.partial(fetch_kernel, which), [shape(x.shape, x.dtype) for x in a], [pltpu.SemaphoreType.DMA((len(a),))],
            place, *a, *b, left_out=range(2 * len(a)), mib=12,
        )

    def linear(here, pieces):
        return in_vmem(
            functools.partial(tick_kernel, False, length, block), [joint, joint] + [piece] * 4,
            [pltpu.VMEM((tp,) + piece.shape, BF16), everything_half], place, *pieces, *here, mib=16,
        )

    def summed(here, upstream, own, got):
        return in_vmem(functools.partial(norm_kernel, length), [piece], [], place, own, *got, here[3], upstream)[0]

    def early():
        return across(n_send), across(hidden)

    both_whole = shape((rows, 2 * channels), BF16)

    def opening():
        def begin():
            both_3, own, *sent = in_vmem(
                functools.partial(tick_kernel, True, length, block), [both_whole] + [wide] * 4,
                [pltpu.VMEM((tp,) + wide.shape, BF16), everything, weight, weight, out_weight_v, pltpu.SemaphoreType.DMA((5,))],
                place, upstream_grad, value_w, gate_w, out_w, mine, other, left_out=(0, 1, 2, 3), mib=28,
            )
            return *in_vmem(
                functools.partial(norm_kernel, length), [piece] * 2, [], place, own, *scattered(sent), mine, other, up_mine, up_other
            ), both_3

        parcel_o = lent(other)
        share_3, share_3o, both_3 = lax.cond(section == last, begin, lambda: untouched(piece, piece, both_whole))
        arrived = jnp.where(core == 1, share_3, swap(share_3o, 1))
        pieces, here = gathered(arrived), fetched(0, parcel_o)
        joint_2, pair_2, own, *sent = linear(here, pieces)
        share_2 = summed(here, arrived, own, scattered(sent))
        return share_2, joint_2, pair_2, share_3, share_3o, both_3, *untouched(parcel, side, tokens)

    def waiting():
        return *untouched(piece, joint, joint, piece, piece, both_whole), lent(other), *early()

    share_2, joint_2, pair_2, share_3, share_3o, both_3, parcel_o, n_got, h_got = lax.cond(section < 2, waiting, opening)
    arrived = swap(share_2, 2)

    def closing(arrived, *_):
        pieces, here = gathered(arrived), fetched(1, parcel_o)
        joint_1, pair_1, own, *sent = linear(here, pieces)
        got = scattered(sent)
        next_here = fetched(0, after(parcel_o, own))
        share_1 = summed(here, arrived, own, after(got, next_here[0]))
        here, pieces = next_here, gathered(share_1)
        joint_1x = across(after(joint_1, share_1))
        pair_1o = swap(after(pair_1, share_1), 1)
        joint_0, pair_0, own, *sent = linear(here, after(pieces, pair_1o))
        joint_0x = across(joint_0)
        got = scattered(sent)
        pair_0o = swap(pair_0, 1)
        share_0 = summed(here, share_1, own, got)
        joint_1o, joint_0o = swap(after(joint_1x, share_0), 1), swap(joint_0x, 1)
        out = []
        for first, second in ((pair_1, pair_0), (pair_1o, pair_0o), (joint_1x, joint_0x), (joint_1o, joint_0o)):
            out += [untouched(joint)[0], first, second]
        return (*out, *untouched(side, tokens), jnp.where(core == 0, share_0, share_1), jnp.where(core == 0, share_1, share_0))

    def hand_over(arrived, share_2, joint_2, pair_2, share_3, share_3o, both_3):
        keep_3, send_3 = in_vmem(functools.partial(pick_kernel, length, block), [side, side], [everything], place, upstream_grad)

        def chosen(whole, rows, half):
            return jnp.where(core == 1, jnp.concatenate([both_3[rows], whole[rows]], axis=0), half)

        mine, other = slice(0, length), slice(length, rows)
        pair_m, pair_o = chosen(keep_3, mine, pair_2), chosen(keep_3, other, swap(pair_2, 1))
        joint_m, joint_o = chosen(send_3, mine, joint_2), chosen(send_3, other, swap(joint_2, 1))
        out = []
        for only in (pair_m, pair_o, across(joint_m), across(joint_o)):
            out += [only, *untouched(joint, joint)]
        return (*out, *early(), jnp.where(core == 1, share_3, share_2), share_2)

    *choices, n_far, h_far, share_m, share_o = lax.cond(
        section < 2, closing, hand_over, arrived, share_2, joint_2, pair_2, share_3, share_3o, both_3
    )
    share_o = swap(share_o, 1)
    share_o = jnp.where(section == last, share_3o, share_o)
    d_share = jnp.concatenate([jnp.where(core == 0, share_m, share_o), jnp.where(core == 0, share_o, share_m)], axis=0)
    factors = (n_keep, hidden, *choices, n_far, n_got, n_got, h_far, h_got, h_got)
    loaded = [
        pltpu.VMEM((2 * rows, 2 * channels), BF16), pltpu.VMEM(side.shape, BF16), pltpu.VMEM(side.shape, BF16),
        pltpu.VMEM(side.shape, BF16), pltpu.VMEM(tokens.shape, BF16), pltpu.SemaphoreType.DMA((10,)),
    ]
    moving = shape((block, 3 * channels), BF16)
    forward, backward = in_vmem(first_kernel, [moving] * 2, loaded, place, *factors, left_out=range(2, 20), mib=12)
    parts, = in_vmem(
        grads_kernel, [shape((layers, block, 3 * channels), BF16)], [pltpu.VMEM((half, 2 * rows), BF16)] + loaded,
        place, *after(factors, forward), left_out=range(2, 20), mib=16,
    )
    backward = after(backward, parts)
    far, near = layers // 2, layers - 1 - layers // 2
    for step in range(far):
        forward = along(forward, 1)
        if step < far - 1:
            forward = in_vmem(functools.partial(ring_kernel, far - 1 - step), [moving], [], place, forward, parts)[0]
        if step < near:
            backward = along(backward, -1)
        if step < near - 1:
            backward = in_vmem(functools.partial(ring_kernel, step + 1 - near), [moving], [], place, backward, parts)[0]
    grads = in_vmem(
        functools.partial(close_kernel, factor), [shape((block, channels), F32)] * 3, [], place, forward, backward, parts,
    )
    return (d_share[None],) + tuple(g[None] for g in grads)


def solution(mesh):
    placed = (
        P("pp", None, "dp", None), P(None, "dp", None), P("pp", None), P("pp", None, "tp"),
        P("pp", None, "tp"), P("pp", "tp", None), P("pp", None, "tp"),
    )
    return jax.shard_map(
        shards, mesh=mesh, in_specs=placed,
        out_specs=(P("pp", None, ("dp", "tp"), None), P("pp", "dp", "tp"), P("pp", "dp", "tp"), P("pp", "dp", "tp")),
        check_vma=False,
    )
```
